128 devices in a mesh: dp: 32 (over z, x, y_hi), mp: 4 (over y_lo, core).
Axes of the slice: x: 4, y: 4 (y_hi: 2, y_lo: 2; y = y_hi * 2 + y_lo), z: 4, core: 2. Of those that a mesh axis runs over, the one named last changes fastest.
Arguments:
- block_input: bfloat16 [12288, 1024], P('dp', 'mp'), may hold values from -6 to 6
- cotangent: bfloat16 [12288, 1024], P('dp', 'mp'), may hold values from -6 to 6
- norm_gain: bfloat16 [1, 2, 1024], P(None, None, 'dp'), may hold values from 0.25 to 1.75
- w_qkv: bfloat16 [1, 1024, 3, 1024], P(None, 'dp', None, 'mp'), may hold values from -0.1875 to 0.1875
- w_out: bfloat16 [1, 1024, 1024], P(None, 'mp', 'dp'), may hold values from -0.75 to 0.75
- w_in: bfloat16 [1, 1024, 2, 2624], P(None, 'dp', None, 'mp'), may hold values from -0.1875 to 0.1875
- w_down: bfloat16 [1, 2624, 1024], P(None, 'mp', 'dp'), may hold values from -0.125 to 0.125
Outputs:
- block_output: bfloat16 [12288, 1024], P('dp', 'mp')
- input_grad: bfloat16 [12288, 1024], P('dp', 'mp')
- gain_grad: float32 [1, 2, 1024], P(None, None, 'dp')
- qkv_grad: float32 [1, 1024, 3, 1024], P(None, 'dp', None, 'mp')
- out_grad: float32 [1, 1024, 1024], P(None, 'mp', 'dp')
- in_grad: float32 [1, 1024, 2, 2624], P(None, 'dp', None, 'mp')
- down_grad: float32 [1, 2624, 1024], P(None, 'mp', 'dp')
The draws below stay inside these ranges and needn't reach their ends.
All inputs are finite; a program needn't handle non-finite values.
Results may differ from the reference program's by a relative error of at most 0.03.
Values may be sent and summed in bfloat16 or wider, within the bound.
No kernel may reach another device: no remote copies, remote signals or barrier semaphores. Data moves between devices by JAX's collectives and lax.ppermute only.
A program may use at most 128 MiB of HBM per device.

```python
import jax
import jax.numpy as jnp
from jax import lax

D = 1024
HEADS = 16
HEAD_DIM = 64
FF = 2624
WINDOW = 128
LEN = 2048
LAYERS = 1
SEQ_B = 1
SEQ_A = 2
TOK_DEV = 384
TOKENS = 12288
N_DP = 32


def level_of(stream_key, dims, cuts, smallest, top_value):
    def one(dim, parts):
        draws = jax.random.uniform(jax.random.fold_in(jax.random.fold_in(stream_key, 6), dim), (parts,), jnp.float32, smallest / len(cuts), top_value / len(cuts))
        return jnp.repeat(jnp.exp(draws), dims[dim] // parts).reshape((-1,) + (1,) * (len(dims) - dim - 1))

    factor_of = one(*cuts[0])
    for cut in cuts[1:]:
        factor_of = factor_of * one(*cut)
    return factor_of


def scatter_about(own_key, shape, width, most, split=(), held_as=jnp.bfloat16):
    level = level_of(own_key, shape, split, -0.22, 0.18) if split else 1.0
    array = jax.random.normal(own_key, shape, jnp.float32) * width * level
    return jnp.minimum(jnp.maximum(array, -most), most).astype(held_as)


def setup_inputs(seed: int = 0) -> dict:
    keys = jax.random.split(jax.random.key(seed), 8)
    return {
        "block_input": scatter_about(keys[0], (TOKENS, D), 1.0, 6.0, ((0, 32), (1, 4))),
        "cotangent": scatter_about(keys[1], (TOKENS, D), 1.0, 6.0, ((0, 32), (1, 4))),
        "norm_gain": jnp.clip(1.0 + 0.15 * jax.random.normal(keys[2], (LAYERS, 2, D), jnp.float32), 0.25, 1.75).astype(jnp.bfloat16),
        "w_qkv": scatter_about(keys[3], (LAYERS, D, 3, D), D ** -0.5, 0.1875, ((1, 32), (3, 4))),
        "w_out": scatter_about(keys[4], (LAYERS, D, D), (D // 16) ** -0.5, 0.75, ((1, 4), (2, 32))),
        "w_in": scatter_about(keys[5], (LAYERS, D, 2, FF), D ** -0.5, 0.1875, ((1, 32), (3, 4))),
        "w_down": scatter_about(keys[6], (LAYERS, FF, D), FF ** -0.5, 0.125, ((1, 4), (2, 32))),
    }


EPS = 1e-05
NEG = -1e+30
TOP = lax.Precision.HIGHEST

@jax.custom_vjp
def low(v):
    return lax.optimization_barrier(v.astype(jnp.bfloat16)).astype(jnp.float32)

@jax.custom_vjp
def low_back(v):
    return v

def low_keep(v):
    return (low(v), None)

def low_pass(kept, grad):
    return (grad,)

def back_keep(v):
    return (v, None)

def back_low(kept, grad):
    return (low(grad),)
low.defvjp(low_keep, low_pass)
low_back.defvjp(back_keep, back_low)

def normalize(stream):
    middle = lax.optimization_barrier(jnp.mean(stream, axis=-1, keepdims=True))
    centred = stream - middle
    spread = lax.optimization_barrier(jnp.mean(centred * centred, axis=-1, keepdims=True))
    return centred * lax.rsqrt(spread + EPS)

def rope_tables(position):
    frequency = 1.0 / 10000.0 ** (jnp.arange(0, HEAD_DIM, 2, dtype=jnp.float32) / HEAD_DIM)
    angles = position.astype(jnp.float32)[:, None] * frequency[None, :]
    angles = jnp.concatenate([angles, angles], axis=-1)
    return (jnp.cos(angles)[:, None, :], jnp.sin(angles)[:, None, :])

def turn(values, cos_table, sin_table):
    middle = values.shape[-1] // 2
    rotated = jnp.concatenate([-values[..., middle:], values[..., :middle]], axis=-1)
    return values * cos_table + rotated * sin_table

def window_attention(triple):
    queries, key_rows, value_rows = triple
    reach = WINDOW // 2
    block = min(512, LEN)
    padding = jnp.zeros((reach, HEADS, HEAD_DIM), jnp.float32)
    keys_padded = jnp.concatenate([padding, key_rows, padding], axis=0)
    values_padded = jnp.concatenate([padding, value_rows, padding], axis=0)

    def one_block(index):
        begin_row = index * block
        query_rows = lax.dynamic_slice_in_dim(queries, begin_row, block, 0)
        key_block = lax.dynamic_slice_in_dim(keys_padded, begin_row, block + 2 * reach, 0)
        value_block = lax.dynamic_slice_in_dim(values_padded, begin_row, block + 2 * reach, 0)
        scores = jnp.einsum('qhd,khd->hqk', query_rows, key_block, precision=TOP) * HEAD_DIM ** (-0.5)
        scores = low_back(scores)
        rows_at = begin_row + jnp.arange(block, dtype=jnp.int32)
        cols_at = begin_row - reach + jnp.arange(block + 2 * reach, dtype=jnp.int32)
        allowed = (jnp.abs(rows_at[:, None] - cols_at[None, :]) <= reach) & (cols_at[None, :] >= 0) & (cols_at[None, :] < LEN)
        scores = jnp.where(allowed[None], scores, NEG)
        weights = low(jax.nn.softmax(scores, axis=-1))
        return jnp.einsum('hqk,khd->qhd', weights, value_block, precision=TOP)
    blocks = lax.map(jax.checkpoint(one_block), jnp.arange(LEN // block, dtype=jnp.int32))
    return blocks.reshape(LEN, HEADS, HEAD_DIM)

def forward(stream_in, gains, w_qkv, w_out, w_in, w_down):
    groups = stream_in.shape[0]
    stream = stream_in.reshape(-1, D)
    cos_table, sin_table = rope_tables(jnp.arange(LEN, dtype=jnp.int32))
    for layer_no in range(LAYERS):
        normed = low(normalize(stream) * gains[layer_no, 0])
        raw = low_back(jnp.einsum('nd,dcf->ncf', normed, w_qkv[layer_no], precision=TOP))
        raw = raw.reshape(groups, LEN, 3, HEADS, HEAD_DIM)
        queries = low(turn(raw[:, :, 0], cos_table, sin_table))
        key_rows = low(turn(raw[:, :, 1], cos_table, sin_table))
        value_rows = low(raw[:, :, 2])
        attended = lax.map(window_attention, (queries, key_rows, value_rows))
        attended = low(low_back(attended.reshape(-1, D)))
        stream = stream + low_back(jnp.dot(attended, w_out[layer_no], precision=TOP))
        normed2 = low(normalize(stream) * gains[layer_no, 1])
        expanded = low_back(jnp.einsum('nd,dcf->ncf', normed2, w_in[layer_no], precision=TOP))
        activated = low(jax.nn.gelu(expanded[:, 0], approximate=False) * expanded[:, 1])
        stream = stream + low_back(jnp.dot(activated, w_down[layer_no], precision=TOP))
    return stream.reshape(stream_in.shape)

def to_sequences(flat, counts):
    blocked = flat.reshape(N_DP, TOK_DEV, flat.shape[-1])
    pieces = []
    offset = 0
    for number in counts:
        rows_here = number * LEN // N_DP
        portion = blocked[:, offset:offset + rows_here]
        pieces.append(portion.reshape(number, LEN, flat.shape[-1]))
        offset = offset + rows_here
    return jnp.concatenate(pieces, axis=0)

def from_sequences(sequences, counts):
    pieces = []
    offset = 0
    for number in counts:
        rows_here = number * LEN // N_DP
        portion = sequences[offset:offset + number]
        pieces.append(portion.reshape(N_DP, rows_here, sequences.shape[-1]))
        offset = offset + number
    return jnp.concatenate(pieces, axis=1).reshape(TOKENS, sequences.shape[-1])

def reference(block_input, cotangent, norm_gain, w_qkv, w_out, w_in, w_down):
    counts = (SEQ_A, SEQ_A, SEQ_B, SEQ_B)
    seq_total = 2 * (SEQ_A + SEQ_B)
    params = (norm_gain.astype(jnp.float32), w_qkv.astype(jnp.float32), w_out.astype(jnp.float32), w_in.astype(jnp.float32), w_down.astype(jnp.float32))
    inputs = to_sequences(block_input.astype(jnp.float32), counts).reshape(seq_total // 2, 2, LEN, D)
    pulled = to_sequences(cotangent.astype(jnp.float32), counts).reshape(seq_total // 2, 2, LEN, D)

    def group_step(totals, item_pair):
        portion, pull_in = item_pair
        result, pullback = jax.vjp(forward, portion, *params)
        grads = pullback(pull_in)
        totals = tuple((left + right for left, right in zip(totals, grads[1:])))
        return (totals, (result, grads[0]))
    zeros = tuple((jnp.zeros_like(member) for member in params))
    totals, (results, input_grads) = lax.scan(group_step, zeros, (inputs, pulled))
    block_output = from_sequences(results.reshape(seq_total, LEN, D), counts).astype(jnp.bfloat16)
    input_grad = from_sequences(input_grads.reshape(seq_total, LEN, D), counts).astype(jnp.bfloat16)
    return (block_output, input_grad, totals[0], totals[1], totals[2], totals[3], totals[4])
```

```python
import functools

import jax
import jax.numpy as jnp
from jax import lax
from jax.experimental import pallas as pl
from jax.experimental.pallas import tpu as pltpu
from jax.sharding import Mesh
from jax.sharding import PartitionSpec as P

HEAD_DIM = 64
REACH = 64
LEN = 2048
EPS = 1e-05
NEG = -1e30
BF = jnp.bfloat16
F32 = jnp.float32

D = 1024
FF = 656
FFP = 768
ROWS = (128, 128, 64, 64)
OWN_AT = (0, 128, 256, 320)
EXT_AT = (0, 256, 512, 704)
OWN = 384
EXT = 896
HALO = 256
NT = (((1,), (1,)), ((), ()))
TN = (((0,), (0,)), ((), ()))


def turn_by(x, axis, by):
    n = lax.axis_size(axis)
    return lax.ppermute(x, axis, [((i + by) % n, i) for i in range(n)])


def gather_parts(x, axis):
    return [x] + [turn_by(x, axis, k) for k in range(1, lax.axis_size(axis))]


def reduce_parts(parts, axis):
    n = lax.axis_size(axis)
    total = parts[0].astype(F32)
    for k in range(1, n):
        total = total + lax.ppermute(
            parts[k].astype(BF), axis, [(i, (i + k) % n) for i in range(n)]
        ).astype(F32)
    return total


def gather_rows(shard, first, last):
    x = jnp.concatenate(gather_parts(shard, "yh"), axis=0)
    x = jnp.concatenate(gather_parts(x, first), axis=0)
    return gather_parts(x, last)


def reduce_rows(parts, first, last):
    x = reduce_parts(parts, first)
    x = x.astype(BF)
    x = reduce_parts([x[k * 64 : k * 64 + 64] for k in range(4)], last)
    x = x.astype(BF)
    return reduce_parts([x[:32], x[32:]], "yh")


def call(body, outs, scratch, *args):
    in_specs = [
        pl.BlockSpec(memory_space=pltpu.SMEM if a.dtype == jnp.int32 else pltpu.VMEM) for a in args
    ]
    return pl.pallas_call(
        body,
        out_shape=[jax.ShapeDtypeStruct(s, t) for s, t in outs],
        in_specs=in_specs,
        out_specs=[pl.BlockSpec(memory_space=pltpu.VMEM)] * len(outs),
        scratch_shapes=[pltpu.VMEM(s, t) for s, t in scratch],
        compiler_params=pltpu.CompilerParams(vmem_limit_bytes=56 * 1024 * 1024),
    )(*args)


def mm(a, b):
    return jnp.dot(a, b, preferred_element_type=F32)


def nt(a, b):
    return lax.dot_general(a, b, NT, preferred_element_type=F32)


def tn(a, b):
    return lax.dot_general(a, b, TN, preferred_element_type=F32)


def turn_matrix(x, y):
    a = lax.broadcasted_iota(jnp.int32, (256, 256), 0)
    r = lax.broadcasted_iota(jnp.int32, (256, 256), 1)
    source = (((x + (r >> 6)) & 3) << 6) | (((y + (r >> 5)) & 1) << 5) | (r & 31)
    return jnp.where(a == source, 1.0, 0.0).astype(BF)


def slot_of(place_ref, k):
    return place_ref[3] ^ ((place_ref[0] + k) & 3)


def enter_kernel(place, x0, x1, x2, x3, c0, c1, c2, c3, xr, xhat, rinv, ct):
    q = turn_matrix(place[1], place[2])
    for k in range(4):
        s = slot_of(place, k)
        cols = slice(k * 256, k * 256 + 256)
        for j in range(4):

            @pl.when(s == j)
            def _(j=j, cols=cols):
                xr[:, cols] = mm((x0, x1, x2, x3)[j][...], q).astype(BF)
                ct[:, cols] = mm((c0, c1, c2, c3)[j][...], q).astype(BF)

    @pl.loop(0, EXT // 128)
    def _(i):
        rows = pl.ds(pl.multiple_of(i * 128, 128), 128)
        v = xr[rows, :].astype(F32)
        v = v - jnp.mean(v, axis=1, keepdims=True)
        r = lax.rsqrt(jnp.mean(v * v, axis=1, keepdims=True) + EPS)
        xhat[rows, :] = v * r
        rinv[rows, :] = jnp.broadcast_to(r, (128, 128))


def spread(parts, full):
    for kx in range(4):
        for kz in range(4):
            at = (kz * 4 + kx) * 64
            full[at : at + 64, :] = parts[kx][kz * 64 : kz * 64 + 64, :]


def half_turn(v):
    low = (lax.broadcasted_iota(jnp.int32, v.shape, 1) & 63) < 32
    return jnp.where(low, pltpu.roll(v, 96, axis=1), pltpu.roll(v, 32, axis=1))


def window(place, b):
    r = ROWS[b]
    i = lax.broadcasted_iota(jnp.int32, (r, r + 128), 0)
    j = lax.broadcasted_iota(jnp.int32, (r, r + 128), 1)
    begin = (place[4] * r) & (LEN - 1)
    at = j + (begin - REACH)
    return (j >= i) & (j <= i + 128) & (at >= 0) & (at < LEN)


def head_lanes(shape, h):
    return (lax.broadcasted_iota(jnp.int32, shape, 1) >> 6) == h


def only(v, h):
    return jnp.where(head_lanes(v.shape, h), v, jnp.zeros_like(v))


def soft(q, k, allowed):
    s = jnp.where(allowed, nt(q, k) * 0.125, NEG)
    e = jnp.exp(s - jnp.max(s, axis=1, keepdims=True))
    return e / jnp.sum(e, axis=1, keepdims=True)


def attend_kernel(
    place, xhat, gain, a0, a1, a2, a3, b0, b1, b2, b3, cos, sin,
    normed, qo, kx, vx, att, wa, wb, wide, nb, raw,
):
    for k, part in enumerate((a0, a1, a2, a3)):
        wa[k * 256 : k * 256 + 256, :] = part[...]
    spread((b0, b1, b2, b3), wb)
    g = gain[...]

    @pl.loop(0, EXT // 128)
    def _(i):
        rows = pl.ds(pl.multiple_of(i * 128, 128), 128)
        nb[rows, :] = (xhat[rows, :] * g).astype(BF)

    for b in range(4):
        e, o, r = EXT_AT[b] + REACH, OWN_AT[b], ROWS[b]
        normed[o : o + r, :] = nb[e : e + r, :]
    for t in range(3):
        raw[...] = mm(nb[...], wa[:, t * 128 : t * 128 + 128])
        if t < 2:
            v = raw[...] * cos[...] + half_turn(raw[...]) * sin[...]
            wide[:, t * 128 : t * 128 + 128] = v.astype(BF)
        else:
            vx[:, 0:128] = raw[...].astype(BF)
    for b in range(4):
        e, o, r = EXT_AT[b] + REACH, OWN_AT[b], ROWS[b]
        qo[o : o + r, :] = wide[e : e + r, :]
    for t in range(3):
        raw[...] = mm(nb[...], wb[:, t * 128 : t * 128 + 128])
        if t < 2:
            v = raw[...] * cos[...] + half_turn(raw[...]) * sin[...]
            kx[:, t * 128 : t * 128 + 128] = v.astype(BF)
        else:
            vx[:, 128:256] = raw[...].astype(BF)
    for b in range(4):
        allowed = window(place, b)
        e, o, r = EXT_AT[b], OWN_AT[b], ROWS[b]
        for t in range(2):
            lanes = slice(t * 128, t * 128 + 128)
            q, k, v = qo[o : o + r, lanes], kx[e : e + r + 128, lanes], vx[e : e + r + 128, lanes]
            p0 = soft(only(q, 0), k, allowed).astype(BF)
            p1 = soft(only(q, 1), k, allowed).astype(BF)
            o0, o1 = mm(p0, v), mm(p1, v)
            att[o : o + r, lanes] = jnp.where(head_lanes(o0.shape, 0), o0, o1).astype(BF)


def mlp_kernel(
    place, xr, t0, t1, t2, t3, oz0, oz1, oz2, oz3, ox0, ox1, ox2, ox3, gain,
    z0, z1, z2, z3, x0, x1, x2, x3, ct,
    stream, xhat, rinv, normed, act, de0, de1, dn, gpart, wo, wz, wx,
    work,
):
    for k, part in enumerate((oz0, oz1, oz2, oz3)):
        wo[k * 256 : k * 256 + 256, 0:512] = part[...]
    for kx in range(4):
        for kz in range(4):
            at = (kz * 4 + kx) * 64
            wo[at : at + 64, 512:1024] = (ox0, ox1, ox2, ox3)[kx][kz * 64 : kz * 64 + 64, :]
    for k, part in enumerate((z0, z1, z2, z3)):
        wz[k * 256 : k * 256 + 256, :] = part[...]
    spread((x0, x1, x2, x3), wx)

    for b in range(4):
        e, o, r = EXT_AT[b] + REACH, OWN_AT[b], ROWS[b]
        stream[o : o + r, :] = xr[e : e + r, :].astype(F32)

    @pl.loop(0, 4)
    def _(n):
        at = pl.ds(pl.multiple_of(n * 256, 256), 256)
        y = nt(t0[...], wo[at, 0:256]) + nt(t1[...], wo[at, 256:512])
        y = y + nt(t2[...], wo[at, 512:768]) + nt(t3[...], wo[at, 768:1024])
        stream[:, at] += y

    @pl.loop(0, OWN // 128)
    def _(i):
        rows = pl.ds(pl.multiple_of(i * 128, 128), 128)
        v = stream[rows, :]
        v = v - jnp.mean(v, axis=1, keepdims=True)
        r = lax.rsqrt(jnp.mean(v * v, axis=1, keepdims=True) + EPS)
        v = v * r
        xhat[rows, :] = v
        rinv[rows, :] = jnp.broadcast_to(r, (128, 128))
        normed[rows, :] = (v * gain[...]).astype(BF)

    @pl.loop(0, FFP // 128)
    def _(n):
        at = pl.ds(pl.multiple_of(n * 128, 128), 128)
        e0 = mm(normed[...], wz[:, at])
        e1 = mm(normed[...], wx[:, at])

        @pl.when(n < 3)
        def _():
            work[...] = mm(ct[...], wz[:, pl.ds(pl.multiple_of(n * 128 + FFP, 128), 128)])

        @pl.when(n >= 3)
        def _():
            work[...] = mm(ct[...], wx[:, pl.ds(pl.multiple_of((n - 3) * 128 + FFP, 128), 128)])

        da = work[...]
        cdf = 0.5 * (1.0 + lax.erf(e0 * 0.7071067811865476))
        pdf = jnp.exp(-0.5 * e0 * e0) * 0.3989422804014327
        ge = e0 * cdf
        act[:, at] = (ge * e1).astype(BF)
        de0[:, at] = (da * e1 * (cdf + e0 * pdf)).astype(BF)
        de1[:, at] = (da * ge).astype(BF)

    for k in range(4):
        at = slice(k * 256, k * 256 + 256)
        y = nt(de0[...], wz[at, 0:FFP]) + nt(de1[...], wx[at, 0:FFP])
        dn[pl.ds(slot_of(place, k), 1)] = y.astype(BF)[None]
        gpart[:, at] = jnp.sum(y * xhat[:, at], axis=0, keepdims=True)


def mlp_grads_kernel(place, normed, act, de0, de1, ct, wz, wx, down, z0, z1, z2, z3, x0, x1, x2, x3):
    gz, gx = (z0, z1, z2, z3), (x0, x1, x2, x3)
    for k in range(4):
        at = slice(k * 256, k * 256 + 256)
        y = nt(act[:, 0:384], wz[at, FFP:]) + nt(act[:, 384:768], wx[at, FFP:])
        down[pl.ds(slot_of(place, k), 1)] = y.astype(BF)[None]
    for k in range(4):
        at = slice(k * 256, k * 256 + 256)
        n, c = normed[:, at], ct[:, at]
        gz[k][:, 0:FFP] = tn(n, de0[...]).astype(BF)
        gz[k][:, FFP:] = tn(c, act[:, 0:384]).astype(BF)
        g = tn(n, de1[...]).astype(BF)
        h = tn(c, act[:, 384:768]).astype(BF)
        for kx in range(4):
            gx[kx][k * 64 : k * 64 + 64, 0:FFP] = g[kx * 64 : kx * 64 + 64]
            gx[kx][k * 64 : k * 64 + 64, FFP:] = h[kx * 64 : kx * 64 + 64]


def attend_back_kernel(
    place, own, other, ct, xhat, rinv, gain, wo, att, qo, kx, vx,
    grad, o0, o1, o2, o3, dq, dk, dv, below, above,
    gb, da, dk_ext, dv_ext,
):
    for k in range(4):
        s = slot_of(place, k)
        at = slice(k * 256, k * 256 + 256)

        @pl.when((s & 1) == 0)
        def _(s=s, at=at):
            grad[:, at] = own[pl.ds(s >> 1, 1)][0].astype(F32)

        @pl.when((s & 1) == 1)
        def _(s=s, at=at):
            grad[:, at] = other[pl.ds(s >> 1, 1)][0].astype(F32)

    @pl.loop(0, OWN // 128)
    def _(i):
        rows = pl.ds(pl.multiple_of(i * 128, 128), 128)
        e = grad[rows, :] * gain[...]
        x = xhat[rows, :]
        m1 = jnp.mean(e, axis=1, keepdims=True)
        m2 = jnp.mean(e * x, axis=1, keepdims=True)
        r = rinv[rows, 0:1]
        g = ct[rows, :].astype(F32) + r * (e - m1 - x * m2)
        grad[rows, :] = g
        gb[rows, :] = g.astype(BF)

    da[...] = mm(gb[...], wo[:, 0:256]).astype(BF)
    dk_ext[...] = jnp.zeros_like(dk_ext)
    dv_ext[...] = jnp.zeros_like(dv_ext)
    for b in range(4):
        allowed = window(place, b)
        e, o, r = EXT_AT[b], OWN_AT[b], ROWS[b]
        for t in range(2):
            lanes = slice(t * 128, t * 128 + 128)
            q, k, v = qo[o : o + r, lanes], kx[e : e + r + 128, lanes], vx[e : e + r + 128, lanes]
            d = da[o : o + r, lanes]
            dqs, dks, dvs = [], [], []
            for h in range(2):
                qh, dh = only(q, h), only(d, h)
                p = soft(qh, k, allowed)
                dp = nt(dh, v)
                ds = (p * (dp - jnp.sum(p * dp, axis=1, keepdims=True))).astype(BF)
                dqs.append(mm(ds, k))
                dks.append(tn(ds, qh))
                dvs.append(tn(p.astype(BF), dh))
            dq[o : o + r, lanes] = jnp.where(head_lanes(dqs[0].shape, 0), dqs[0], dqs[1]) * 0.125
            dk_ext[e : e + r + 128, lanes] = (dks[0] + dks[1]) * 0.125
            dv_ext[e : e + r + 128, lanes] = dvs[0] + dvs[1]
    for b in range(4):
        e, o, r = EXT_AT[b], OWN_AT[b], ROWS[b]
        dk[o : o + r, :] = dk_ext[e + 64 : e + 64 + r, :]
        dv[o : o + r, :] = dv_ext[e + 64 : e + 64 + r, :]
        at = slice(b * 64, b * 64 + 64)
        below[at, 0:256] = dk_ext[e : e + 64, :].astype(BF)
        below[at, 256:512] = dv_ext[e : e + 64, :].astype(BF)
        above[at, 0:256] = dk_ext[e + 64 + r : e + 128 + r, :].astype(BF)
        above[at, 256:512] = dv_ext[e + 64 + r : e + 128 + r, :].astype(BF)
    for k in range(4):
        (o0, o1, o2, o3)[k][...] = tn(gb[:, k * 256 : k * 256 + 256], att[...]).astype(BF)


def qkv_back_kernel(
    place, dq, dk, dv, low, high, cos, sin, xhat, gain, normed,
    a0, a1, a2, a3, b0, b1, b2, b3,
    dn, stats, gpart, z0, z1, z2, z3, x0, x1, x2, x3,
    ra, rb, wb,
):
    spread((b0, b1, b2, b3), wb)
    for b in range(4):
        o, r = OWN_AT[b], ROWS[b]
        at = slice(b * 64, b * 64 + 64)
        dk[o : o + 64, :] += low[at, 0:256].astype(F32)
        dv[o : o + 64, :] += low[at, 256:512].astype(F32)
        dk[o + r - 64 : o + r, :] += high[at, 0:256].astype(F32)
        dv[o + r - 64 : o + r, :] += high[at, 256:512].astype(F32)
    for b in range(4):
        e, o, r = EXT_AT[b] + REACH, OWN_AT[b], ROWS[b]
        c, s = cos[e : e + r, :], sin[e : e + r, :]
        for t in range(2):
            lanes = slice(t * 128, t * 128 + 128)
            v = dq[o : o + r, lanes]
            ra[o : o + r, lanes] = (v * c - half_turn(v) * s).astype(BF)
            v = dk[o : o + r, lanes]
            rb[o : o + r, lanes] = (v * c - half_turn(v) * s).astype(BF)
    ra[:, 256:384] = dv[:, 0:128].astype(BF)
    rb[:, 256:384] = dv[:, 128:256].astype(BF)
    m1 = jnp.zeros((OWN, 1), F32)
    m2 = jnp.zeros((OWN, 1), F32)
    for k in range(4):
        at = slice(k * 256, k * 256 + 256)
        y = nt(ra[...], (a0, a1, a2, a3)[k][...]) + nt(rb[...], wb[at, :])
        dn[pl.ds(slot_of(place, k), 1)] = y.astype(BF)[None]
        e = y * gain[:, at]
        acc = jnp.zeros((1, 256), F32)
        for b in range(4):
            ee, o, r = EXT_AT[b] + REACH, OWN_AT[b], ROWS[b]
            acc = acc + jnp.sum(y[o : o + r] * xhat[ee : ee + r, at], axis=0, keepdims=True)
        gpart[:, at] = acc
        xk = jnp.concatenate(
            [xhat[EXT_AT[b] + REACH : EXT_AT[b] + REACH + ROWS[b], at] for b in range(4)], axis=0
        )
        m1 = m1 + jnp.sum(e, axis=1, keepdims=True)
        m2 = m2 + jnp.sum(e * xk, axis=1, keepdims=True)
    lane = lax.broadcasted_iota(jnp.int32, (OWN, 128), 1)
    stats[...] = jnp.where(lane == 0, m1, jnp.where(lane == 1, m2, 0.0)) * (1.0 / D)
    gz, gx = (z0, z1, z2, z3), (x0, x1, x2, x3)
    for k in range(4):
        at = slice(k * 256, k * 256 + 256)
        gz[k][...] = tn(normed[:, at], ra[...]).astype(BF)
        g = tn(normed[:, at], rb[...]).astype(BF)
        for kx in range(4):
            gx[kx][k * 64 : k * 64 + 64, :] = g[kx * 64 : kx * 64 + 64]


def leave_kernel(place, grad, dn_a, dn_b, stats_a, stats_b, xhat, rinv, gain, out):
    q = turn_matrix(place[1], place[2])
    m1 = stats_a[:, 0:1] + stats_b[:, 0:1]
    m2 = stats_a[:, 1:2] + stats_b[:, 1:2]
    dn = dn_a[...].astype(F32) + dn_b[...].astype(F32)
    for k in range(4):

        @pl.when(slot_of(place, k) == 0)
        def _(k=k):
            at = slice(k * 256, k * 256 + 256)
            e = dn * gain[:, at]
            for b in range(4):
                ee, o, r = EXT_AT[b] + REACH, OWN_AT[b], ROWS[b]
                rows = slice(o, o + r)
                x = xhat[ee : ee + r, at]
                y = grad[rows, at] + rinv[ee : ee + r, 0:1] * (e[rows] - m1[rows] - x * m2[rows])
                out[rows, :] = nt(y.astype(BF), q).astype(BF)


def output_kernel(place, stream, a, b, out):
    q = turn_matrix(place[1], place[2])
    for k in range(4):

        @pl.when(slot_of(place, k) == 0)
        def _(k=k):
            y = stream[:, k * 256 : k * 256 + 256] + a[...].astype(F32) + b[...].astype(F32)
            out[...] = nt(y.astype(BF), q).astype(BF)


def mp_gather(x):
    far = turn_by(x, "yl", 1)
    return x, turn_by(x, "c", 1), far, turn_by(far, "c", 1)


def mp_reduce(slots):
    got = turn_by(slots[1::2], "c", 1)
    return (slots[0::2].astype(F32) + got.astype(F32)).astype(BF)


def dp_turn(x, by):
    pairs = [(i, i + by) for i in range(32) if 0 <= i + by < 32]
    return lax.ppermute(x, ("z", "x", "yh"), pairs)


def rows_of(x, low, high):
    parts = []
    for b in range(4):
        o, r = OWN_AT[b], ROWS[b]
        parts += [low[b * 64 : b * 64 + 64], x[o : o + r], high[b * 64 : b * 64 + 64]]
    return jnp.concatenate(parts, axis=0)


def gains_in_order(gain):
    g = jnp.concatenate(gather_parts(gain, "yh"), axis=1)
    g = jnp.concatenate(gather_parts(g, "x"), axis=1)
    return jnp.concatenate(gather_parts(g, "z"), axis=1).astype(F32)


def gains_back(g):
    def step(v, axis, n):
        w = v.shape[1] // n
        total = v[:, :w]
        for k in range(1, n):
            total = total + lax.ppermute(
                v[:, k * w : k * w + w], axis, [(i, (i + k) % n) for i in range(n)]
            )
        return total

    g = g + turn_by(g, "c", 1)
    g = g + turn_by(g, "yl", 1)
    return step(step(step(g, "z", 4), "x", 4), "yh", 2)


def rope_tables(place):
    rows = []
    for b in range(4):
        r = ROWS[b]
        rows.append((place * r + jnp.arange(r + 128, dtype=jnp.int32) - REACH) % LEN)
    position = jnp.concatenate(rows).astype(F32)
    frequency = 1.0 / 10000.0 ** (jnp.arange(0, HEAD_DIM, 2, dtype=F32) / HEAD_DIM)
    angles = position[:, None] * frequency[None, :]
    c, s = jnp.cos(angles), jnp.sin(angles)
    return jnp.concatenate([c, c, c, c], axis=1), jnp.concatenate([-s, s, -s, s], axis=1)


def body(block_input, cotangent, norm_gain, w_qkv, w_out, w_in, w_down):
    z, x, y = lax.axis_index("z"), lax.axis_index("x"), lax.axis_index("yh")
    mp = lax.axis_index("yl") * 2 + lax.axis_index("c")
    dp = (z * 4 + x) * 2 + y
    place = jnp.stack([z, x, y, mp, dp]).astype(jnp.int32)

    q, k, v = w_qkv[0, :, 0], w_qkv[0, :, 1], w_qkv[0, :, 2]
    shard_a = jnp.concatenate([q, v[:, :128]], axis=1)
    shard_b = jnp.concatenate([k, v[:, 128:]], axis=1)
    out_t = jnp.concatenate(mp_gather(w_out[0].T), axis=1)
    pad = ((0, 0), (0, FFP - FF))
    down_t = jnp.pad(w_down[0].T, pad)
    shard_z = jnp.concatenate([jnp.pad(w_in[0, :, 0], pad), down_t[:, :384]], axis=1)
    shard_x = jnp.concatenate([jnp.pad(w_in[0, :, 1], pad), down_t[:, 384:]], axis=1)

    a = gather_rows(shard_a, "x", "z")
    b = gather_rows(shard_b, "z", "x")
    gains = gains_in_order(norm_gain[0])
    lows = jnp.concatenate([block_input[o + r - 64 : o + r] for o, r in zip(OWN_AT, ROWS)], axis=0)
    highs = jnp.concatenate([block_input[o : o + 64] for o in OWN_AT], axis=0)
    x_ext = rows_of(block_input, dp_turn(lows, 1), dp_turn(highs, -1))
    x_slots = mp_gather(x_ext)
    c_slots = mp_gather(cotangent)
    oz = gather_rows(out_t[:, :512], "x", "z")
    ox = gather_rows(out_t[:, 512:], "z", "x")
    wz = gather_rows(shard_z, "x", "z")
    wx = gather_rows(shard_x, "z", "x")
    cos, sin = rope_tables(dp)

    xr, xhat1, rinv1, ct = call(
        enter_kernel,
        [((EXT, D), BF), ((EXT, D), F32), ((EXT, 128), F32), ((OWN, D), BF)],
        [],
        place, *x_slots, *c_slots,
    )
    normed1, qo, kx, vx, att = call(
        attend_kernel,
        [((OWN, D), BF), ((OWN, 256), BF), ((EXT, 256), BF), ((EXT, 256), BF), ((OWN, 256), BF)],
        [((D, 384), BF), ((D, 384), BF), ((EXT, 256), BF), ((EXT, D), BF), ((EXT, 128), F32)],
        place, xhat1, gains[0:1], *a, *b, cos, sin,
    )
    att_slots = mp_gather(att)
    (stream, xhat2, rinv2, normed2, act, de0, de1, dn2, gain2, wo, wz_full, wx_full) = call(
        mlp_kernel,
        [
            ((OWN, D), F32), ((OWN, D), F32), ((OWN, 128), F32), ((OWN, D), BF),
            ((OWN, FFP), BF), ((OWN, FFP), BF), ((OWN, FFP), BF),
            ((4, OWN, 256), BF), ((1, D), F32),
            ((D, D), BF), ((D, FFP + 384), BF), ((D, FFP + 384), BF),
        ],
        [((OWN, 128), F32)],
        place, xr, *att_slots, *oz, *ox, gains[1:2], *wz, *wx, ct,
    )
    half = mp_reduce(dn2)
    half = (half.astype(F32) + turn_by(half, "yl", 1)[::-1].astype(F32)).astype(BF)
    other = turn_by(half, "c", 1)

    down, *g = call(
        mlp_grads_kernel,
        [((4, OWN, 256), BF)] + [((256, FFP + 384), BF)] * 8,
        [],
        place, normed2, act, de0, de1, ct, wz_full, wx_full,
    )
    grad_z = reduce_rows(g[:4], "z", "x")
    grad_x = reduce_rows(g[4:], "x", "z")
    down_half = mp_reduce(down)
    (block_output,) = call(
        output_kernel, [((OWN, 256), BF)], [], place, stream, down_half[0], turn_by(down_half[1], "yl", 1)
    )

    grad, o0, o1, o2, o3, dq, dk, dv, below, above = call(
        attend_back_kernel,
        [((OWN, D), F32)] + [((256, 256), BF)] * 4
        + [((OWN, 256), F32)] * 3 + [((HALO, 512), BF)] * 2,
        [((OWN, D), BF), ((OWN, 256), BF), ((EXT, 256), F32), ((EXT, 256), F32)],
        place, half, other, ct, xhat2, rinv2, gains[1:2], wo, att, qo, kx, vx,
    )
    low = dp_turn(above, 1)
    high = dp_turn(below, -1)
    grad_out = reduce_rows([o0, o1, o2, o3], "z", "x")
    dn1, stats, gain1, *g = call(
        functools.partial(qkv_in_place, qkv_back_kernel),
        [((4, OWN, 256), BF), ((OWN, 128), F32), ((1, D), F32)] + [((256, 384), BF)] * 8,
        [((OWN, 384), BF), ((OWN, 384), BF), ((D, 384), BF), ((OWN, 256), F32), ((OWN, 256), F32)],
        place, dq, dk, dv, low, high, cos, sin, xhat1, gains[0:1], normed1, *a, *b,
    )
    grad_a = reduce_rows(g[:4], "z", "x")
    grad_b = reduce_rows(g[4:], "x", "z")
    half = mp_reduce(dn1)
    stats = stats + turn_by(stats, "c", 1)
    (input_grad,) = call(
        leave_kernel, [((OWN, 256), BF)], [],
        place, grad, half[0], turn_by(half[1], "yl", 1), stats, turn_by(stats, "yl", 1),
        xhat1, rinv1, gains[0:1],
    )
    gain_grad = gains_back(jnp.concatenate([gain1, gain2], axis=0))

    qkv_grad = jnp.stack(
        [grad_a[:, :256], grad_b[:, :256], jnp.concatenate([grad_a[:, 256:], grad_b[:, 256:]], axis=1)],
        axis=1,
    )
    in_grad = jnp.stack([grad_z[:, :FF], grad_x[:, :FF]], axis=1)
    down_grad = jnp.concatenate([grad_z[:, FFP:], grad_x[:, FFP : FFP + FF - 384]], axis=1).T
    return (
        block_output, input_grad, gain_grad[None], qkv_grad[None], grad_out.T[None],
        in_grad[None], down_grad[None],
    )


def qkv_in_place(inner, place, dq, dk, dv, *refs):
    *refs, dks, dvs = refs
    dks[...] = dk[...]
    dvs[...] = dv[...]
    inner(place, dq, dks, dvs, *refs)


def solution(mesh):
    fine = Mesh(mesh.devices.reshape(4, 4, 2, 2, 2), ("z", "x", "yh", "yl", "c"))
    dp, mp = ("z", "x", "yh"), ("yl", "c")
    return jax.shard_map(
        body,
        mesh=fine,
        in_specs=(
            P(dp, mp),
            P(dp, mp),
            P(None, None, dp),
            P(None, dp, None, mp),
            P(None, mp, dp),
            P(None, dp, None, mp),
            P(None, mp, dp),
        ),
        out_specs=(
            P(dp, mp),
            P(dp, mp),
            P(None, None, dp),
            P(None, dp, None, mp),
            P(None, mp, dp),
            P(None, dp, None, mp),
            P(None, mp, dp),
        ),
        check_vma=False,
    )
```

```python
import functools

import jax
import jax.numpy as jnp
from jax import lax
from jax.experimental import pallas as pl
from jax.experimental.pallas import tpu as pltpu
from jax.sharding import Mesh
from jax.sharding import PartitionSpec as P

HEAD_DIM = 64
REACH = 64
LEN = 2048
EPS = 1e-05
NEG = -1e30
BF = jnp.bfloat16
F32 = jnp.float32
DP = ("z", "x", "yh")

D = 1024
FF = 656
MAIN = 640
TAIL = 16
FFP = 768
VMEM_MB = 56
PACK = 1024 + 384
ROWS = (128, 128, 64, 64)
OWN_AT = (0, 128, 256, 320)
EXT_AT = (0, 256, 512, 704)
OWN = 384
EXT = 896
HALO = 256
NT = (((1,), (1,)), ((), ()))
TN = (((0,), (0,)), ((), ()))


def turn_by(x, axis, by):
    n = lax.axis_size(axis)
    return lax.ppermute(x, axis, [((i + by) % n, i) for i in range(n)])


def sum_of(got, n):
    return jnp.sum(got.reshape(n, got.shape[0] // n, -1).astype(F32), axis=0)


def scatter_sum(x, axis):
    return lax.psum_scatter(x, axis, scatter_dimension=0, tiled=True)


def columns(full, at, width):
    return full, pl.BlockSpec((full.shape[0], width), lambda i: (0, at))


def call(us, body, outs, scratch, *args):
    specs = []
    for a in args:
        if isinstance(a, tuple):
            specs.append(a[1])
        else:
            where = pltpu.SMEM if a.dtype == jnp.int32 else pltpu.VMEM
            specs.append(pl.BlockSpec(memory_space=where))
    return pl.pallas_call(
        body,
        grid=(1,),
        out_shape=[jax.ShapeDtypeStruct(s, t) for s, t in outs],
        in_specs=specs,
        out_specs=[pl.BlockSpec(memory_space=pltpu.VMEM)] * len(outs),
        scratch_shapes=[pltpu.VMEM(s, t) for s, t in scratch],
        cost_estimate=pl.CostEstimate(flops=us * 10**9, bytes_accessed=0, transcendentals=0),
        compiler_params=pltpu.CompilerParams(vmem_limit_bytes=VMEM_MB * 1024 * 1024),
    )(*[a[0] if isinstance(a, tuple) else a for a in args])


def mm(a, b):
    return jnp.dot(a, b, preferred_element_type=F32)


def nt(a, b):
    return lax.dot_general(a, b, NT, preferred_element_type=F32)


def tn(a, b):
    return lax.dot_general(a, b, TN, preferred_element_type=F32)


def block(place, s):
    return pl.ds(pl.multiple_of((place[0] ^ s) * 256, 256), 256)


def enter_kernel(place, x0, x1, x2, x3, xr, own, stats):
    for s in range(4):
        at, x = block(place, s), (x0, x1, x2, x3)[s]
        own[:, at] = x[0:OWN, :]
        for b in range(4):
            e, o, r = EXT_AT[b], OWN_AT[b], ROWS[b]
            xr[e : e + 64, at] = x[OWN + b * 64 : OWN + b * 64 + 64, :]
            xr[e + 64 : e + 64 + r, at] = x[o : o + r, :]
            k = OWN + HALO + b * 64
            xr[e + 64 + r : e + 128 + r, at] = x[k : k + 64, :]

    @pl.loop(0, EXT // 128)
    def _(i):
        rows = pl.ds(pl.multiple_of(i * 128, 128), 128)
        v = xr[rows, :].astype(F32)
        m = jnp.mean(v, axis=1, keepdims=True)
        v = v - m
        r = lax.rsqrt(jnp.mean(v * v, axis=1, keepdims=True) + EPS)
        lane = lax.broadcasted_iota(jnp.int32, (128, 128), 1)
        stats[rows, :] = jnp.where(lane == 0, m, r)


def normalized(x, stats):
    return (x.astype(F32) - stats[:, 0:1]) * stats[:, 1:2]


def own_rows(ref):
    return jnp.concatenate(
        [ref[EXT_AT[b] + REACH : EXT_AT[b] + REACH + ROWS[b], :] for b in range(4)], axis=0
    )


def load_sum(place, half, far, half_c, far_c, full):
    for s in range(4):
        a, b = ((half, far), (half_c, far_c))[s & 1]
        full[:, block(place, s)] = a[s >> 1].astype(F32) + b[1 - (s >> 1)].astype(F32)


def half_turn(v):
    low = (lax.broadcasted_iota(jnp.int32, v.shape, 1) & 63) < 32
    return jnp.where(low, pltpu.roll(v, 96, axis=1), pltpu.roll(v, 32, axis=1))


def window(place, b):
    r = ROWS[b]
    i = lax.broadcasted_iota(jnp.int32, (r, r + 128), 0)
    j = lax.broadcasted_iota(jnp.int32, (r, r + 128), 1)
    begin = (place[1] * r) & (LEN - 1)
    at = j + (begin - REACH)
    return (j >= i) & (j <= i + 128) & (at >= 0) & (at < LEN)


def head_lanes(shape, h):
    return (lax.broadcasted_iota(jnp.int32, shape, 1) >> 6) == h


def only(v, h):
    return jnp.where(head_lanes(v.shape, h), v, jnp.zeros_like(v))


def attend_kernel(
    place, xr, stat, w, cos, sin,
    gains, normed, qo, kx, vx, att, lse, even, odd, wide, nb, raw,
):
    gains[...] = w[:, 1024:1152].astype(F32).T[0:8]
    g = gains[0:1]

    @pl.loop(0, EXT // 128)
    def _(i):
        rows = pl.ds(pl.multiple_of(i * 128, 128), 128)
        nb[rows, :] = (normalized(xr[rows, :], stat[rows, :]) * g).astype(BF)

    for b in range(4):
        e, o, r = EXT_AT[b] + REACH, OWN_AT[b], ROWS[b]
        normed[o : o + r, :] = nb[e : e + r, :]
    for t in range(3):
        into = (wide, kx, vx)[t]
        raw[...] = mm(nb[...], w[:, t * 256 : t * 256 + 256])
        for h in range(2):
            lanes = slice(h * 128, h * 128 + 128)
            v = raw[:, lanes]
            if t < 2:
                v = v * cos[...] + half_turn(v) * sin[...]
            into[:, lanes] = v.astype(BF)
    for b in range(4):
        e, o, r = EXT_AT[b] + REACH, OWN_AT[b], ROWS[b]
        qo[o : o + r, :] = wide[e : e + r, :]
    for b in range(4):
        allowed = window(place, b)
        e, at, r = EXT_AT[b], OWN_AT[b], ROWS[b]
        lane = lax.broadcasted_iota(jnp.int32, (r, 128), 1)
        kept = jnp.zeros((r, 128), F32)
        for t in range(2):
            lanes = slice(t * 128, t * 128 + 128)
            q, k, v = qo[at : at + r, lanes], kx[e : e + r + 128, lanes], vx[e : e + r + 128, lanes]
            o = []
            for h in range(2):
                x = jnp.where(allowed, nt(only(q, h), k) * 0.125, NEG)
                most = jnp.max(x, axis=1, keepdims=True)
                x = jnp.exp(x - most)
                total = jnp.sum(x, axis=1, keepdims=True)
                o.append(mm((x * (1.0 / total)).astype(BF), v))
                kept = jnp.where(lane == t * 2 + h, most + jnp.log(total), kept)
            att[at : at + r, lanes] = jnp.where(head_lanes(o[0].shape, 0), o[0], o[1]).astype(BF)
        lse[at : at + r, :] = kept
    for s in range(4):
        y = nt(att[...], w[block(place, s), 768:1024])
        (even, odd)[s & 1][s >> 1] = y.astype(BF)


def tail_of(tail, k):
    v = tail.astype(F32)
    v = v if k == 0 else pltpu.roll(v, 128 - k * TAIL, axis=1)
    lane = lax.broadcasted_iota(jnp.int32, v.shape, 1)
    return jnp.where(lane < TAIL, v, 0.0).astype(BF)


def mlp_kernel(
    place, xo, half, far, half_c, far_c, gains, w, c0, c1, c2, c3,
    ct, own, xhat, rinv, normed, act, de0, de1, even, odd, gpart,
    w0, w1, wd, stream,
):
    for s in range(4):
        ct[:, block(place, s)] = (c0, c1, c2, c3)[s][...]
    tail = w[:, 3 * MAIN :]
    for k, full in enumerate((w0, w1, wd)):
        full[:, 0:MAIN] = w[:, k * MAIN : k * MAIN + MAIN]
        full[:, MAIN:] = tail_of(tail, k)

    gain = gains[1:2]
    load_sum(place, half, far, half_c, far_c, stream)
    stream[...] += xo[...].astype(F32)
    own[...] = stream[:, block(place, 0)]

    @pl.loop(0, OWN // 128)
    def _(i):
        rows = pl.ds(pl.multiple_of(i * 128, 128), 128)
        v = stream[rows, :]
        v = v - jnp.mean(v, axis=1, keepdims=True)
        r = lax.rsqrt(jnp.mean(v * v, axis=1, keepdims=True) + EPS)
        v = v * r
        xhat[rows, :] = v
        rinv[rows, :] = jnp.broadcast_to(r, (128, 128))
        normed[rows, :] = (v * gain).astype(BF)

    @pl.loop(0, FFP // 256)
    def _(n):
        at = pl.ds(pl.multiple_of(n * 256, 256), 256)
        e0 = mm(normed[...], w0[:, at])
        e1 = mm(normed[...], w1[:, at])
        da = mm(ct[...], wd[:, at])
        cdf = 0.5 * (1.0 + lax.erf(e0 * 0.7071067811865476))
        pdf = jnp.exp(-0.5 * e0 * e0) * 0.3989422804014327
        ge = e0 * cdf
        act[:, at] = (ge * e1).astype(BF)
        de0[:, at] = (da * e1 * (cdf + e0 * pdf)).astype(BF)
        de1[:, at] = (da * ge).astype(BF)

    for s in range(4):
        at = block(place, s)
        y = nt(de0[...], w0[at, :]) + nt(de1[...], w1[at, :])
        (even, odd)[s & 1][s >> 1] = y.astype(BF)
        gpart[:, at] = jnp.sum(y * xhat[:, at], axis=0, keepdims=True)


def mlp_grads_kernel(place, normed, act, de0, de1, ct, wm, wt, down, g, wd):
    wd[:, 0:MAIN] = wm[...]
    wd[:, MAIN:] = tail_of(wt[...], 2)
    for s in range(4):
        down[s] = nt(act[...], wd[block(place, s), :]).astype(BF)
    lane = lax.broadcasted_iota(jnp.int32, (256, 128), 1)
    for k in range(4):
        at = slice(k * 256, k * 256 + 256)
        n, c = normed[:, at], ct[:, at]
        y0, y1, y2 = tn(n, de0[...]), tn(n, de1[...]), tn(c, act[...])
        tail = jnp.zeros((256, 128), F32)
        for t, y in enumerate((y0, y1, y2)):
            end = jnp.where(lane < TAIL, y[:, MAIN:], 0.0)
            tail = tail + (end if t == 0 else pltpu.roll(end, t * TAIL, axis=1))
        for t, y in enumerate((y0, y1, y2)):
            g[at, t * MAIN : t * MAIN + MAIN] = y[:, 0:MAIN].astype(BF)
        g[at, 3 * MAIN :] = tail.astype(BF)


def attend_back_kernel(
    place, half, far, half_c, far_c, ct, xhat, rinv, gains, w, att, qo, kx, vx, lse,
    own, go, dq, dk, dv, below, above,
    grad, gb, da, dk_ext, dv_ext,
):
    gain = gains[1:2]
    load_sum(place, half, far, half_c, far_c, grad)

    @pl.loop(0, OWN // 128)
    def _(i):
        rows = pl.ds(pl.multiple_of(i * 128, 128), 128)
        e = grad[rows, :] * gain
        x = xhat[rows, :]
        m1 = jnp.mean(e, axis=1, keepdims=True)
        m2 = jnp.mean(e * x, axis=1, keepdims=True)
        r = rinv[rows, 0:1]
        g = ct[rows, :].astype(F32) + r * (e - m1 - x * m2)
        grad[rows, :] = g
        gb[rows, :] = g.astype(BF)

    own[...] = grad[:, block(place, 0)]
    da[...] = mm(gb[...], w[...]).astype(BF)
    dk_ext[...] = jnp.zeros_like(dk_ext)
    dv_ext[...] = jnp.zeros_like(dv_ext)
    for b in range(4):
        allowed = window(place, b)
        e, o, r = EXT_AT[b], OWN_AT[b], ROWS[b]
        for t in range(2):
            lanes = slice(t * 128, t * 128 + 128)
            q, k, v = qo[o : o + r, lanes], kx[e : e + r + 128, lanes], vx[e : e + r + 128, lanes]
            d = da[o : o + r, lanes]
            dqs, dks, dvs = [], [], []
            for h in range(2):
                qh, dh = only(q, h), only(d, h)
                total = lse[o : o + r, t * 2 + h : t * 2 + h + 1]
                p = jnp.exp(jnp.where(allowed, nt(qh, k) * 0.125 - total, NEG))
                dp = nt(dh, v)
                ds = (p * (dp - jnp.sum(p * dp, axis=1, keepdims=True))).astype(BF)
                dqs.append(mm(ds, k))
                dks.append(tn(ds, qh))
                dvs.append(tn(p.astype(BF), dh))
            dq[o : o + r, lanes] = jnp.where(head_lanes(dqs[0].shape, 0), dqs[0], dqs[1]) * 0.125
            dk_ext[e : e + r + 128, lanes] = (dks[0] + dks[1]) * 0.125
            dv_ext[e : e + r + 128, lanes] = dvs[0] + dvs[1]
    for b in range(4):
        e, o, r = EXT_AT[b], OWN_AT[b], ROWS[b]
        dk[o : o + r, :] = dk_ext[e + 64 : e + 64 + r, :]
        dv[o : o + r, :] = dv_ext[e + 64 : e + 64 + r, :]
        at = slice(b * 64, b * 64 + 64)
        below[at, 0:256] = dk_ext[e : e + 64, :].astype(BF)
        below[at, 256:512] = dv_ext[e : e + 64, :].astype(BF)
        above[at, 0:256] = dk_ext[e + 64 + r : e + 128 + r, :].astype(BF)
        above[at, 256:512] = dv_ext[e + 64 + r : e + 128 + r, :].astype(BF)
    for k in range(4):
        go[k * 256 : k * 256 + 256, :] = tn(gb[:, k * 256 : k * 256 + 256], att[...]).astype(BF)


def qkv_back_kernel(
    place, dq, dk, dv, low, high, cos, sin, xo, stat, gains, gain2, w,
    dn, pack, xq, raw, gsum,
):
    for b in range(4):
        o, r = OWN_AT[b], ROWS[b]
        at = slice(b * 64, b * 64 + 64)
        dk[o : o + 64, :] += low[at, 0:256].astype(F32)
        dv[o : o + 64, :] += low[at, 256:512].astype(F32)
        dk[o + r - 64 : o + r, :] += high[at, 0:256].astype(F32)
        dv[o + r - 64 : o + r, :] += high[at, 256:512].astype(F32)
    for b in range(4):
        e, o, r = EXT_AT[b] + REACH, OWN_AT[b], ROWS[b]
        c, s = cos[e : e + r, :], sin[e : e + r, :]
        for t in range(2):
            lanes = slice(t * 128, t * 128 + 128)
            v = dq[o : o + r, lanes]
            raw[o : o + r, lanes] = (v * c - half_turn(v) * s).astype(BF)
            v = dk[o : o + r, lanes]
            lanes = slice(256 + t * 128, 256 + t * 128 + 128)
            raw[o : o + r, lanes] = (v * c - half_turn(v) * s).astype(BF)
    raw[:, 512:768] = dv[...].astype(BF)
    st = own_rows(stat)
    m1 = jnp.zeros((OWN, 1), F32)
    m2 = jnp.zeros((OWN, 1), F32)
    for s in range(4):
        at = block(place, s)
        y = nt(raw[...], w[at, :])
        dn[s] = y.astype(BF)
        x = normalized(xo[:, at], st)
        if s == 0:
            xq[...] = x
        e = y * gains[0:1, at]
        m1 = m1 + jnp.sum(e, axis=1, keepdims=True)
        m2 = m2 + jnp.sum(e * x, axis=1, keepdims=True)
        gsum[:, at] = jnp.sum(y * x, axis=0, keepdims=True)
    lane = lax.broadcasted_iota(jnp.int32, (OWN, 128), 1)
    sums = jnp.where(lane == 0, m1, jnp.where(lane == 1, m2, 0.0)) * (1.0 / D)
    pack[:, D:] = sums.T[0:8]
    pack[0:1, 0:D] = gsum[...]
    pack[1:2, 0:D] = gain2[...]


def qkv_grads_kernel(normed, raw, go, p0, p1, p2, p3, g):
    for k in range(4):
        at = slice(k * 256, k * 256 + 256)
        g[at, 0:768] = tn(normed[:, at], raw[...]).astype(BF)
    g[:, 768:1024] = go[...]
    row = lax.broadcasted_iota(jnp.int32, (8, D), 0)
    both = jnp.where(row < 2, p0[:, :D] + p1[:, :D] + p2[:, :D] + p3[:, :D], 0.0)
    g[:, 1024:1152] = jnp.concatenate([both, jnp.zeros((120, D), F32)], axis=0).T.astype(BF)


def leave_kernel(place, grad, own, a, b, c, p0, p1, p2, p3, xq, stat, gains, out):
    sums = p0[:, D:] + p1[:, D:] + p2[:, D:] + p3[:, D:]
    sums = jnp.concatenate([sums, jnp.zeros((120, OWN), F32)], axis=0).T
    m1, m2 = sums[:, 0:1], sums[:, 1:2]
    e = own[0].astype(F32) + a[...].astype(F32) + b[...].astype(F32) + c[...].astype(F32)
    e = e * gains[0:1, block(place, 0)]
    y = grad[...] + own_rows(stat)[:, 1:2] * (e - m1 - xq[...] * m2)
    out[...] = y.astype(BF)


def output_kernel(stream, own, a, b, c, out):
    y = stream[...] + own[0].astype(F32) + a[...].astype(F32)
    out[...] = (y + b[...].astype(F32) + c[...].astype(F32)).astype(BF)


def mp_gather(x):
    far = turn_by(x, "yl", 1)
    return x, turn_by(x, "c", 1), far, turn_by(far, "c", 1)


def mp_turn(x, slot):
    return lax.ppermute(x, ("yl", "c"), [(i, i ^ slot) for i in range(4)])


def mp_terms(slots):
    return [slots, *(mp_turn(slots[s], s) for s in (1, 2, 3))]


def mp_reduce(even, odd):
    return (even.astype(F32) + turn_by(odd, "c", 1).astype(F32)).astype(BF)


def mp_sum(even, odd):
    half = mp_reduce(even, odd)
    far = turn_by(half, "yl", 1)
    return half, far, turn_by(half, "c", 1), turn_by(far, "c", 1)


def dp_turn(x, by):
    pairs = [(i, i + by) for i in range(32) if 0 <= i + by < 32]
    return lax.ppermute(x, ("z", "x", "yh"), pairs)


def rope_tables(place):
    rows = []
    for b in range(4):
        r = ROWS[b]
        rows.append((place * r + jnp.arange(r + 128, dtype=jnp.int32) - REACH) % LEN)
    position = jnp.concatenate(rows).astype(F32)
    frequency = 1.0 / 10000.0 ** (jnp.arange(0, HEAD_DIM, 2, dtype=F32) / HEAD_DIM)
    angles = position[:, None] * frequency[None, :]
    c, s = jnp.cos(angles), jnp.sin(angles)
    return jnp.concatenate([c, c, c, c], axis=1), jnp.concatenate([-s, s, -s, s], axis=1)


def body(block_input, cotangent, norm_gain, w_qkv, w_out, w_in, w_down):
    mp = lax.axis_index("yl") * 2 + lax.axis_index("c")
    dp = (lax.axis_index("z") * 4 + lax.axis_index("x")) * 2 + lax.axis_index("yh")
    place = jnp.stack([mp, dp]).astype(jnp.int32)

    gain_t = jnp.pad(norm_gain[0].T, ((0, 0), (0, 126)))
    shard0 = jnp.concatenate([w_qkv[0].reshape(32, 768), w_out[0].T, gain_t], axis=1)
    in0, in1, down_t = w_in[0, :, 0], w_in[0, :, 1], w_down[0].T
    shard1 = jnp.concatenate(
        [in0[:, :MAIN], in1[:, :MAIN], down_t[:, :MAIN]]
        + [in0[:, MAIN:], in1[:, MAIN:], down_t[:, MAIN:], jnp.zeros((32, 128 - 3 * TAIL), BF)],
        axis=1,
    )
    shard = jnp.concatenate([shard0, shard1], axis=1)
    lows = jnp.concatenate([block_input[o + r - 64 : o + r] for o, r in zip(OWN_AT, ROWS)], axis=0)
    highs = jnp.concatenate([block_input[o : o + 64] for o in OWN_AT], axis=0)
    low, high = dp_turn(lows, 1), dp_turn(highs, -1)
    shard, low, high = lax.optimization_barrier((shard, low, high))
    pair = turn_by(shard, "yh", 1)
    first = lax.axis_index("yh") == 0
    pair = [jnp.where(first, shard, pair), jnp.where(first, pair, shard)]
    pair = jnp.concatenate(pair, axis=0)
    spread = jnp.broadcast_to(pair[None, :, :1152], (16, 64, 1152)).reshape(D, 1152)
    w0 = lax.all_to_all(spread, ("z", "x"), 0, 0, tiled=True)
    w1 = lax.all_gather(pair[:, 1152:], ("z", "x"), axis=0, tiled=True)
    x_slots = mp_gather(jnp.concatenate([block_input, low, high], axis=0))
    cos, sin = rope_tables(dp)

    xr, xo, stat1 = call(
        5, enter_kernel, [((EXT, D), BF), ((OWN, D), BF), ((EXT, 128), F32)], [], place, *x_slots
    )
    xr, cotangent = lax.optimization_barrier((xr, cotangent))
    xr, *c_slots = lax.optimization_barrier((xr, *mp_gather(cotangent)))
    slots = [((2, OWN, 256), BF)] * 2
    gains, normed1, qo, kx, vx, att, lse, *parts = call(
        10,
        attend_kernel,
        [((8, D), F32), ((OWN, D), BF), ((OWN, 256), BF), ((EXT, 256), BF), ((EXT, 256), BF)]
        + [((OWN, 256), BF), ((OWN, 128), F32)] + slots,
        [((EXT, 256), BF), ((EXT, D), BF), ((EXT, 256), F32)],
        place, xr, stat1, w0, cos, sin,
    )
    ct, stream, xhat2, rinv2, normed2, act, de0, de1, even, odd, gain2 = call(
        10,
        mlp_kernel,
        [
            ((OWN, D), BF), ((OWN, 256), F32), ((OWN, D), F32), ((OWN, 128), F32), ((OWN, D), BF),
            ((OWN, FFP), BF), ((OWN, FFP), BF), ((OWN, FFP), BF),
            *slots, ((1, D), F32),
        ],
        [((D, FFP), BF), ((D, FFP), BF), ((D, FFP), BF), ((OWN, D), F32)],
        place, xo, *mp_sum(*parts), gains, w1, *c_slots,
    )
    half = mp_reduce(even, odd)
    far = turn_by(half, "yl", 1)
    half_c = turn_by(half, "c", 1)
    down, g1 = call(
        9,
        mlp_grads_kernel,
        [((4, OWN, 256), BF), ((D, 2048), BF)],
        [((D, FFP), BF)],
        place, normed2, act, de0, de1, ct, columns(w1, 2, MAIN), columns(w1, 15, 128),
    )
    far, down, g1 = lax.optimization_barrier((far, down, g1))
    far_c = turn_by(far, "c", 1)
    g1 = scatter_sum(g1, "z")
    down = mp_terms(down)

    grad, go, dq, dk, dv, below, above = call(
        11,
        attend_back_kernel,
        [((OWN, 256), F32), ((D, 256), BF)] + [((OWN, 256), F32)] * 3 + [((HALO, 512), BF)] * 2,
        [((OWN, D), F32), ((OWN, D), BF), ((OWN, 256), BF), ((EXT, 256), F32), ((EXT, 256), F32)],
        place, half, far, half_c, far_c, ct, xhat2, rinv2, gains, columns(w0, 3, 256),
        att, qo, kx, vx, lse,
    )
    below, above, *down = lax.optimization_barrier((below, above, *down))
    low = dp_turn(above, 1)
    high = dp_turn(below, -1)
    (block_output,) = call(2, output_kernel, [((OWN, 256), BF)], [], stream, *down)
    dn, pack, xq, raw = call(
        7,
        functools.partial(qkv_in_place, qkv_back_kernel),
        [((4, OWN, 256), BF), ((8, PACK), F32), ((OWN, 256), F32), ((OWN, 768), BF)],
        [((OWN, 256), F32), ((OWN, 256), F32), ((1, D), F32)],
        place, dq, dk, dv, low, high, cos, sin, xo, stat1, gains, gain2, columns(w0, 0, 768),
    )
    dn = mp_terms(dn)
    packs = [pack, *(mp_turn(pack, s) for s in (1, 2, 3))]
    raw, g1, *rest = lax.optimization_barrier((raw, g1, *dn, *packs))
    dn, packs = rest[:4], rest[4:]
    g1 = scatter_sum(g1, "x")
    (g0,) = call(4, qkv_grads_kernel, [((D, 1152), BF)], [], normed1, raw, go, *packs)
    g0 = sum_of(lax.all_to_all(g0, DP, 0, 0, tiled=True), 32)
    (input_grad,) = call(
        2, leave_kernel, [((OWN, 256), BF)], [],
        place, grad, *dn, *packs, xq, stat1, gains,
    )
    g1 = jnp.where(first, g1[:32], g1[32:]).astype(F32) + turn_by(
        jnp.where(first, g1[32:], g1[:32]), "yh", 1
    ).astype(F32)
    in0, in1, down_t = [
        jnp.concatenate(
            [g1[:, k * MAIN : k * MAIN + MAIN], g1[:, 3 * MAIN + k * TAIL : 3 * MAIN + k * TAIL + TAIL]],
            axis=1,
        )
        for k in range(3)
    ]
    return (
        block_output, input_grad, g0[:, 1024:1026].T[None], g0[:, :768].reshape(1, 32, 3, 256),
        g0[:, 768:1024].T[None], jnp.stack([in0, in1], axis=1)[None], down_t.T[None],
    )


def qkv_in_place(inner, place, dq, dk, dv, *refs):
    *refs, dks, dvs, gsum = refs
    dks[...] = dk[...]
    dvs[...] = dv[...]
    inner(place, dq, dks, dvs, *refs, gsum)


def solution(mesh):
    fine = Mesh(mesh.devices.reshape(4, 4, 2, 2, 2), ("z", "x", "yh", "yl", "c"))
    dp, mp = ("z", "x", "yh"), ("yl", "c")
    return jax.shard_map(
        body,
        mesh=fine,
        in_specs=(
            P(dp, mp),
            P(dp, mp),
            P(None, None, dp),
            P(None, dp, None, mp),
            P(None, mp, dp),
            P(None, dp, None, mp),
            P(None, mp, dp),
        ),
        out_specs=(
            P(dp, mp),
            P(dp, mp),
            P(None, None, dp),
            P(None, dp, None, mp),
            P(None, mp, dp),
            P(None, dp, None, mp),
            P(None, mp, dp),
        ),
        check_vma=False,
    )
```

```python
import functools

import jax
import jax.numpy as jnp
from jax import lax
from jax.experimental import pallas as pl
from jax.experimental.pallas import tpu as pltpu
from jax.sharding import Mesh
from jax.sharding import PartitionSpec as P

HEAD_DIM = 64
REACH = 64
LEN = 2048
EPS = 1e-05
NEG = -1e30
BF = jnp.bfloat16
F32 = jnp.float32
DP = ("z", "x", "yh")

D = 1024
FF = 656
MAIN = 640
TAIL = 16
FFP = 768
VMEM_MB = 62
PACK = 1024 + 384
ROWS = (128, 128, 64, 64)
OWN_AT = (0, 128, 256, 320)
EXT_AT = (0, 256, 512, 704)
OWN = 384
EXT = 896
HALO = 256
NT = (((1,), (1,)), ((), ()))
TN = (((0,), (0,)), ((), ()))


def turn_by(x, axis, by):
    n = lax.axis_size(axis)
    return lax.ppermute(x, axis, [((i + by) % n, i) for i in range(n)])


def sum_of(got, n):
    return jnp.sum(got.reshape(n, got.shape[0] // n, -1).astype(F32), axis=0)


def scatter_sum(x, axis):
    return lax.psum_scatter(x, axis, scatter_dimension=0, tiled=True)


def columns(full, at, width):
    return full, pl.BlockSpec((full.shape[0], width), lambda i: (0, at))


def call(us, body, outs, scratch, *args):
    specs = []
    for a in args:
        if isinstance(a, tuple):
            specs.append(a[1])
        else:
            where = pltpu.SMEM if a.dtype == jnp.int32 else pltpu.VMEM
            specs.append(pl.BlockSpec(memory_space=where))
    return pl.pallas_call(
        body,
        grid=(1,),
        out_shape=[jax.ShapeDtypeStruct(s, t) for s, t in outs],
        in_specs=specs,
        out_specs=[pl.BlockSpec(memory_space=pltpu.VMEM)] * len(outs),
        scratch_shapes=[pltpu.VMEM(s, t) for s, t in scratch],
        cost_estimate=pl.CostEstimate(flops=us * 10**9, bytes_accessed=0, transcendentals=0),
        compiler_params=pltpu.CompilerParams(vmem_limit_bytes=VMEM_MB * 1024 * 1024),
    )(*[a[0] if isinstance(a, tuple) else a for a in args])


def mm(a, b):
    return jnp.dot(a, b, preferred_element_type=F32)


def nt(a, b):
    return lax.dot_general(a, b, NT, preferred_element_type=F32)


def tn(a, b):
    return lax.dot_general(a, b, TN, preferred_element_type=F32)


def block(place, s):
    return pl.ds(pl.multiple_of((place[0] ^ s) * 256, 256), 256)


def enter_kernel(place, x0, x1, x2, x3, xr, own, stats):
    for s in range(4):
        at, x = block(place, s), (x0, x1, x2, x3)[s]
        own[:, at] = x[0:OWN, :]
        for b in range(4):
            e, o, r = EXT_AT[b], OWN_AT[b], ROWS[b]
            xr[e : e + 64, at] = x[OWN + b * 64 : OWN + b * 64 + 64, :]
            xr[e + 64 : e + 64 + r, at] = x[o : o + r, :]
            k = OWN + HALO + b * 64
            xr[e + 64 + r : e + 128 + r, at] = x[k : k + 64, :]

    @pl.loop(0, EXT // 128)
    def _(i):
        rows = pl.ds(pl.multiple_of(i * 128, 128), 128)
        v = xr[rows, :].astype(F32)
        m = jnp.mean(v, axis=1, keepdims=True)
        v = v - m
        r = lax.rsqrt(jnp.mean(v * v, axis=1, keepdims=True) + EPS)
        lane = lax.broadcasted_iota(jnp.int32, (128, 128), 1)
        stats[rows, :] = jnp.where(lane == 0, m, r)


def normalized(x, stats):
    return (x.astype(F32) - stats[:, 0:1]) * stats[:, 1:2]


def own_rows(ref):
    return jnp.concatenate(
        [ref[EXT_AT[b] + REACH : EXT_AT[b] + REACH + ROWS[b], :] for b in range(4)], axis=0
    )


def load_sum(place, half, far, half_c, far_c, full):
    for s in range(4):
        a, b = ((half, far), (half_c, far_c))[s & 1]
        full[:, block(place, s)] = a[s >> 1].astype(F32) + b[1 - (s >> 1)].astype(F32)


def half_turn(v):
    low = (lax.broadcasted_iota(jnp.int32, v.shape, 1) & 63) < 32
    return jnp.where(low, pltpu.roll(v, 96, axis=1), pltpu.roll(v, 32, axis=1))


def window(place, b, times):
    r = ROWS[b]
    i = lax.broadcasted_iota(jnp.int32, (times * r, r + 128), 0) & (r - 1)
    j = lax.broadcasted_iota(jnp.int32, (times * r, r + 128), 1)
    begin = (place[1] * r) & (LEN - 1)
    at = j + (begin - REACH)
    return (j >= i) & (j <= i + 128) & (at >= 0) & (at < LEN)


def head_lanes(shape, h):
    return (lax.broadcasted_iota(jnp.int32, shape, 1) >> 6) == h


def only(v, h):
    return jnp.where(head_lanes(v.shape, h), v, jnp.zeros_like(v))


def by_head(v):
    return jnp.concatenate([only(v, h) for h in range(4)], axis=0)


def join_heads(v, r):
    out = v[0:r]
    for h in range(1, 4):
        out = jnp.where(head_lanes(out.shape, h), v[h * r : h * r + r], out)
    return out


def columns_of(v, first, r):
    return jnp.concatenate([v[:, first + h : first + h + 1] for h in range(4)], axis=0)


def attend_kernel(
    place, xr, stat, w, cos, sin,
    gains, normed, qx, kx, vx, att, lse, even, odd, nb, raw,
):
    gains[...] = w[:, 1024:1152].astype(F32).T[0:8]
    g = gains[0:1]

    @pl.loop(0, EXT // 128)
    def _(i):
        rows = pl.ds(pl.multiple_of(i * 128, 128), 128)
        nb[rows, :] = (normalized(xr[rows, :], stat[rows, :]) * g).astype(BF)

    for b in range(4):
        e, o, r = EXT_AT[b] + REACH, OWN_AT[b], ROWS[b]
        normed[o : o + r, :] = nb[e : e + r, :]
    for t in range(3):
        into = (qx, kx, vx)[t]
        raw[...] = mm(nb[...], w[:, t * 256 : t * 256 + 256])
        for h in range(2):
            lanes = slice(h * 128, h * 128 + 128)
            v = raw[:, lanes]
            if t < 2:
                v = v * cos[...] + half_turn(v) * sin[...]
            into[:, lanes] = v.astype(BF)
    for b in range(4):
        e, at, r = EXT_AT[b], OWN_AT[b], ROWS[b]
        allowed = window(place, b, 4)
        x = nt(by_head(qx[e + 64 : e + 64 + r, :]), kx[e : e + r + 128, :]) * 0.125
        x = jnp.where(allowed, x, NEG)
        most = jnp.max(x, axis=1, keepdims=True)
        x = jnp.exp(x - most)
        total = jnp.sum(x, axis=1, keepdims=True)
        y = mm((x * (1.0 / total)).astype(BF), vx[e : e + r + 128, :])
        att[at : at + r, :] = join_heads(y, r).astype(BF)
        total = most + jnp.log(total)
        lane = lax.broadcasted_iota(jnp.int32, (r, 128), 1)
        kept = jnp.zeros((r, 128), F32)
        for h in range(4):
            kept = jnp.where(lane == h, total[h * r : h * r + r], kept)
        lse[at : at + r, :] = kept
    for s in range(4):
        y = nt(att[...], w[block(place, s), 768:1024])
        (even, odd)[s & 1][s >> 1] = y.astype(BF)


def tail_of(tail, k):
    v = tail.astype(F32)
    v = v if k == 0 else pltpu.roll(v, 128 - k * TAIL, axis=1)
    lane = lax.broadcasted_iota(jnp.int32, v.shape, 1)
    return jnp.where(lane < TAIL, v, 0.0).astype(BF)


def mlp_kernel(
    place, xo, half, far, half_c, far_c, gains, w, c0, c1, c2, c3,
    ct, own, xhat, rinv, normed, act, de0, de1, even, odd, gpart,
    w0, w1, wd, stream,
):
    for s in range(4):
        ct[:, block(place, s)] = (c0, c1, c2, c3)[s][...]
    tail = w[:, 3 * MAIN :]
    for k, full in enumerate((w0, w1, wd)):
        full[:, 0:MAIN] = w[:, k * MAIN : k * MAIN + MAIN]
        full[:, MAIN:] = tail_of(tail, k)

    gain = gains[1:2]
    load_sum(place, half, far, half_c, far_c, stream)
    stream[...] += xo[...].astype(F32)
    own[...] = stream[:, block(place, 0)]

    @pl.loop(0, OWN // 128)
    def _(i):
        rows = pl.ds(pl.multiple_of(i * 128, 128), 128)
        v = stream[rows, :]
        v = v - jnp.mean(v, axis=1, keepdims=True)
        r = lax.rsqrt(jnp.mean(v * v, axis=1, keepdims=True) + EPS)
        v = v * r
        xhat[rows, :] = v
        rinv[rows, :] = jnp.broadcast_to(r, (128, 128))
        normed[rows, :] = (v * gain).astype(BF)

    @pl.loop(0, FFP // 256)
    def _(n):
        at = pl.ds(pl.multiple_of(n * 256, 256), 256)
        e0 = mm(normed[...], w0[:, at])
        e1 = mm(normed[...], w1[:, at])
        da = mm(ct[...], wd[:, at])
        cdf = 0.5 * (1.0 + lax.erf(e0 * 0.7071067811865476))
        pdf = jnp.exp(-0.5 * e0 * e0) * 0.3989422804014327
        ge = e0 * cdf
        act[:, at] = (ge * e1).astype(BF)
        de0[:, at] = (da * e1 * (cdf + e0 * pdf)).astype(BF)
        de1[:, at] = (da * ge).astype(BF)

    for s in range(4):
        at = block(place, s)
        y = nt(de0[...], w0[at, :]) + nt(de1[...], w1[at, :])
        (even, odd)[s & 1][s >> 1] = y.astype(BF)
        gpart[:, at] = jnp.sum(y * xhat[:, at], axis=0, keepdims=True)


def mlp_grads_kernel(place, normed, act, de0, de1, ct, wm, wt, down, g, wd):
    wd[:, 0:MAIN] = wm[...]
    wd[:, MAIN:] = tail_of(wt[...], 2)
    for s in range(4):
        down[s] = nt(act[...], wd[block(place, s), :]).astype(BF)
    lane = lax.broadcasted_iota(jnp.int32, (256, 128), 1)
    for k in range(4):
        at = slice(k * 256, k * 256 + 256)
        n, c = normed[:, at], ct[:, at]
        y0, y1, y2 = tn(n, de0[...]), tn(n, de1[...]), tn(c, act[...])
        tail = jnp.zeros((256, 128), F32)
        for t, y in enumerate((y0, y1, y2)):
            end = jnp.where(lane < TAIL, y[:, MAIN:], 0.0)
            tail = tail + (end if t == 0 else pltpu.roll(end, t * TAIL, axis=1))
        for t, y in enumerate((y0, y1, y2)):
            g[at, t * MAIN : t * MAIN + MAIN] = y[:, 0:MAIN].astype(BF)
        g[at, 3 * MAIN :] = tail.astype(BF)


def edges(ref, last):
    at = [OWN_AT[b] + (ROWS[b] - 64 if last else 0) for b in range(4)]
    return jnp.concatenate([ref[k : k + 64, :] for k in at], axis=0)


def norm_back_kernel(
    place, half, far, half_c, far_c, ct, xhat, rinv, gains, w, att, lse,
    own, gb, da, da_first, da_last,
    grad, stat,
):
    gain = gains[1:2]
    load_sum(place, half, far, half_c, far_c, grad)

    @pl.loop(0, OWN // 128)
    def _(i):
        rows = pl.ds(pl.multiple_of(i * 128, 128), 128)
        e = grad[rows, :] * gain
        x = xhat[rows, :]
        m1 = jnp.mean(e, axis=1, keepdims=True)
        m2 = jnp.mean(e * x, axis=1, keepdims=True)
        r = rinv[rows, 0:1]
        g = ct[rows, :].astype(F32) + r * (e - m1 - x * m2)
        grad[rows, :] = g
        gb[rows, :] = g.astype(BF)

    own[...] = grad[:, block(place, 0)]
    da[...] = mm(gb[...], w[...]).astype(BF)
    prod = da[...].astype(F32) * att[...].astype(F32)
    lane = lax.broadcasted_iota(jnp.int32, (OWN, 128), 1)
    kept = lse[...]
    for h in range(4):
        centre = jnp.sum(only(prod, h), axis=1, keepdims=True)
        kept = jnp.where(lane == 4 + h, centre, kept)
    stat[...] = kept
    for out, last in ((da_first, False), (da_last, True)):
        out[0:HALO, :] = edges(da, last)
        st = edges(stat, last).T[0:8]
        high = st.astype(BF)
        rest = (st - high.astype(F32)).astype(BF)
        out[HALO : HALO + 16, :] = jnp.concatenate([high.astype(F32), rest.astype(F32)], axis=0).astype(BF)


def attend_back_kernel(place, da, lse, gb, att, qx, kx, vx, go, dq, dk, dv):
    for b in range(4):
        e, o, r = EXT_AT[b], OWN_AT[b], ROWS[b]
        q, d = by_head(qx[e + 64 : e + 64 + r, :]), by_head(da[o : o + r, :])
        k, v = kx[e : e + r + 128, :], vx[e : e + r + 128, :]
        total = columns_of(lse[o : o + r, :], 0, r)
        p = jnp.exp(jnp.where(window(place, b, 4), nt(q, k) * 0.125 - total, NEG))
        dp = nt(d, v)
        ds = (p * (dp - jnp.sum(p * dp, axis=1, keepdims=True))).astype(BF)
        dq[o : o + r, :] = join_heads(mm(ds, k), r) * 0.125
        dk[o : o + r, :] = tn(ds, q)[64 : 64 + r] * 0.125
        dv[o : o + r, :] = tn(p.astype(BF), d)[64 : 64 + r]
    for k in range(4):
        go[k * 256 : k * 256 + 256, :] = tn(gb[:, k * 256 : k * 256 + 256], att[...]).astype(BF)


def qkv_back_kernel(
    place, dq, dk, dv, da_lo, da_hi, qx, kx, vx, cos, sin, xo, stat, gains, gain2, w,
    dn, pack, xq, raw, gsum,
):
    i = lax.broadcasted_iota(jnp.int32, (256, 64), 0) & 63
    j = lax.broadcasted_iota(jnp.int32, (256, 64), 1)
    pad = jnp.zeros((120, HALO), F32)
    known = []
    for ref in (da_lo, da_hi):
        st = ref[HALO : HALO + 16, :].astype(F32)
        known.append(jnp.concatenate([st[0:8] + st[8:16], pad], axis=0).T)
    for b in range(4):
        e, o, r = EXT_AT[b], OWN_AT[b], ROWS[b]
        begin = (place[1] * r) & (LEN - 1)
        at = slice(b * 64, b * 64 + 64)
        for side in range(2):
            of = e if side == 0 else e + 64 + r
            keys = e + 64 if side == 0 else e + r
            to = slice(o, o + 64) if side == 0 else slice(o + r - 64, o + r)
            allowed = (j <= i) & (begin != 0) if side == 0 else (j >= i) & (begin + r != LEN)
            q, d = by_head(qx[of : of + 64, :]), by_head((da_lo, da_hi)[side][at, :])
            k, v = kx[keys : keys + 64, :], vx[keys : keys + 64, :]
            st = known[side][at]
            p = jnp.exp(jnp.where(allowed, nt(q, k) * 0.125 - columns_of(st, 0, 64), NEG))
            ds = (p * (nt(d, v) - columns_of(st, 4, 64))).astype(BF)
            dk[to, :] += tn(ds, q) * 0.125
            dv[to, :] += tn(p.astype(BF), d)
    for b in range(4):
        e, o, r = EXT_AT[b] + REACH, OWN_AT[b], ROWS[b]
        c, s = cos[e : e + r, :], sin[e : e + r, :]
        for t in range(2):
            lanes = slice(t * 128, t * 128 + 128)
            v = dq[o : o + r, lanes]
            raw[o : o + r, lanes] = (v * c - half_turn(v) * s).astype(BF)
            v = dk[o : o + r, lanes]
            lanes = slice(256 + t * 128, 256 + t * 128 + 128)
            raw[o : o + r, lanes] = (v * c - half_turn(v) * s).astype(BF)
    raw[:, 512:768] = dv[...].astype(BF)
    st = own_rows(stat)
    m1 = jnp.zeros((OWN, 1), F32)
    m2 = jnp.zeros((OWN, 1), F32)
    for s in range(4):
        at = block(place, s)
        y = nt(raw[...], w[at, :])
        dn[s] = y.astype(BF)
        x = normalized(xo[:, at], st)
        if s == 0:
            xq[...] = x
        e = y * gains[0:1, at]
        m1 = m1 + jnp.sum(e, axis=1, keepdims=True)
        m2 = m2 + jnp.sum(e * x, axis=1, keepdims=True)
        gsum[:, at] = jnp.sum(y * x, axis=0, keepdims=True)
    lane = lax.broadcasted_iota(jnp.int32, (OWN, 128), 1)
    sums = jnp.where(lane == 0, m1, jnp.where(lane == 1, m2, 0.0)) * (1.0 / D)
    pack[:, D:] = sums.T[0:8]
    pack[0:1, 0:D] = gsum[...]
    pack[1:2, 0:D] = gain2[...]


def qkv_grads_kernel(normed, raw, go, p0, p1, p2, p3, g):
    for k in range(4):
        at = slice(k * 256, k * 256 + 256)
        g[at, 0:768] = tn(normed[:, at], raw[...]).astype(BF)
    g[:, 768:1024] = go[...]
    row = lax.broadcasted_iota(jnp.int32, (8, D), 0)
    both = jnp.where(row < 2, p0[:, :D] + p1[:, :D] + p2[:, :D] + p3[:, :D], 0.0)
    g[:, 1024:1152] = jnp.concatenate([both, jnp.zeros((120, D), F32)], axis=0).T.astype(BF)


def leave_kernel(place, grad, own, a, b, c, p0, p1, p2, p3, xq, stat, gains, out):
    sums = p0[:, D:] + p1[:, D:] + p2[:, D:] + p3[:, D:]
    sums = jnp.concatenate([sums, jnp.zeros((120, OWN), F32)], axis=0).T
    m1, m2 = sums[:, 0:1], sums[:, 1:2]
    e = own[0].astype(F32) + a[...].astype(F32) + b[...].astype(F32) + c[...].astype(F32)
    e = e * gains[0:1, block(place, 0)]
    y = grad[...] + own_rows(stat)[:, 1:2] * (e - m1 - xq[...] * m2)
    out[...] = y.astype(BF)


def output_kernel(stream, own, a, b, c, out):
    y = stream[...] + own[0].astype(F32) + a[...].astype(F32)
    out[...] = (y + b[...].astype(F32) + c[...].astype(F32)).astype(BF)


def mp_gather(x):
    far = turn_by(x, "yl", 1)
    return x, turn_by(x, "c", 1), far, turn_by(far, "c", 1)


def mp_turn(x, slot):
    return lax.ppermute(x, ("yl", "c"), [(i, i ^ slot) for i in range(4)])


def mp_terms(slots):
    return [slots, *(mp_turn(slots[s], s) for s in (1, 2, 3))]


def mp_reduce(even, odd):
    return (even.astype(F32) + turn_by(odd, "c", 1).astype(F32)).astype(BF)


def mp_sum(even, odd):
    half = mp_reduce(even, odd)
    far = turn_by(half, "yl", 1)
    return half, far, turn_by(half, "c", 1), turn_by(far, "c", 1)


def dp_turn(x, by):
    pairs = [(i, i + by) for i in range(32) if 0 <= i + by < 32]
    return lax.ppermute(x, ("z", "x", "yh"), pairs)


def rope_tables(place):
    rows = []
    for b in range(4):
        r = ROWS[b]
        rows.append((place * r + jnp.arange(r + 128, dtype=jnp.int32) - REACH) % LEN)
    position = jnp.concatenate(rows).astype(F32)
    frequency = 1.0 / 10000.0 ** (jnp.arange(0, HEAD_DIM, 2, dtype=F32) / HEAD_DIM)
    angles = position[:, None] * frequency[None, :]
    c, s = jnp.cos(angles), jnp.sin(angles)
    return jnp.concatenate([c, c, c, c], axis=1), jnp.concatenate([-s, s, -s, s], axis=1)


def body(block_input, cotangent, norm_gain, w_qkv, w_out, w_in, w_down):
    mp = lax.axis_index("yl") * 2 + lax.axis_index("c")
    dp = (lax.axis_index("z") * 4 + lax.axis_index("x")) * 2 + lax.axis_index("yh")
    place = jnp.stack([mp, dp]).astype(jnp.int32)

    gain_t = jnp.pad(norm_gain[0].T, ((0, 0), (0, 126)))
    shard0 = jnp.concatenate([w_qkv[0].reshape(32, 768), w_out[0].T, gain_t], axis=1)
    in0, in1, down_t = w_in[0, :, 0], w_in[0, :, 1], w_down[0].T
    shard1 = jnp.concatenate(
        [in0[:, :MAIN], in1[:, :MAIN], down_t[:, :MAIN]]
        + [in0[:, MAIN:], in1[:, MAIN:], down_t[:, MAIN:], jnp.zeros((32, 128 - 3 * TAIL), BF)],
        axis=1,
    )
    shard = jnp.concatenate([shard0, shard1], axis=1)
    lows = jnp.concatenate([block_input[o + r - 64 : o + r] for o, r in zip(OWN_AT, ROWS)], axis=0)
    highs = jnp.concatenate([block_input[o : o + 64] for o in OWN_AT], axis=0)
    lows, highs, shard = lax.optimization_barrier((lows, highs, shard))
    low, high = dp_turn(lows, 1), dp_turn(highs, -1)
    pair = turn_by(shard, "yh", 1)
    low, high, pair = lax.optimization_barrier((low, high, pair))
    first = lax.axis_index("yh") == 0
    pair = [jnp.where(first, shard, pair), jnp.where(first, pair, shard)]
    pair = jnp.concatenate(pair, axis=0)
    spread = jnp.broadcast_to(pair[None, :, :1152], (16, 64, 1152)).reshape(D, 1152)
    w0 = lax.all_to_all(spread, ("z", "x"), 0, 0, tiled=True)
    w1 = lax.all_gather(pair[:, 1152:], ("z", "x"), axis=0, tiled=True)
    x_slots = mp_gather(jnp.concatenate([block_input, low, high], axis=0))
    cos, sin = rope_tables(dp)

    xr, xo, stat1 = call(
        5, enter_kernel, [((EXT, D), BF), ((OWN, D), BF), ((EXT, 128), F32)], [], place, *x_slots
    )
    xr, cotangent = lax.optimization_barrier((xr, cotangent))
    xr, *c_slots = lax.optimization_barrier((xr, *mp_gather(cotangent)))
    slots = [((2, OWN, 256), BF)] * 2
    gains, normed1, qx, kx, vx, att, lse, *parts = call(
        10,
        attend_kernel,
        [((8, D), F32), ((OWN, D), BF), ((EXT, 256), BF), ((EXT, 256), BF), ((EXT, 256), BF)]
        + [((OWN, 256), BF), ((OWN, 128), F32)] + slots,
        [((EXT, D), BF), ((EXT, 256), F32)],
        place, xr, stat1, w0, cos, sin,
    )
    ct, stream, xhat2, rinv2, normed2, act, de0, de1, even, odd, gain2 = call(
        10,
        mlp_kernel,
        [
            ((OWN, D), BF), ((OWN, 256), F32), ((OWN, D), F32), ((OWN, 128), F32), ((OWN, D), BF),
            ((OWN, FFP), BF), ((OWN, FFP), BF), ((OWN, FFP), BF),
            *slots, ((1, D), F32),
        ],
        [((D, FFP), BF), ((D, FFP), BF), ((D, FFP), BF), ((OWN, D), F32)],
        place, xo, *mp_sum(*parts), gains, w1, *c_slots,
    )
    half = mp_reduce(even, odd)
    far = turn_by(half, "yl", 1)
    half_c = turn_by(half, "c", 1)
    down, g1 = call(
        9,
        mlp_grads_kernel,
        [((4, OWN, 256), BF), ((D, 2048), BF)],
        [((D, FFP), BF)],
        place, normed2, act, de0, de1, ct, columns(w1, 2, MAIN), columns(w1, 15, 128),
    )
    far, down, g1 = lax.optimization_barrier((far, down, g1))
    far_c = turn_by(far, "c", 1)
    g1 = scatter_sum(g1, "z")
    down = mp_terms(down)

    grad, gb, da, da_first, da_last = call(
        6,
        norm_back_kernel,
        [((OWN, 256), F32), ((OWN, D), BF), ((OWN, 256), BF)]
        + [((HALO + 16, 256), BF)] * 2,
        [((OWN, D), F32), ((OWN, 128), F32)],
        place, half, far, half_c, far_c, ct, xhat2, rinv2, gains, columns(w0, 3, 256), att, lse,
    )
    gb, *down = lax.optimization_barrier((gb, *down))
    da_lo, da_hi = dp_turn(da_last, 1), dp_turn(da_first, -1)
    go, dq, dk, dv = call(
        8,
        attend_back_kernel,
        [((D, 256), BF)] + [((OWN, 256), F32)] * 3,
        [],
        place, da, lse, gb, att, qx, kx, vx,
    )
    (block_output,) = call(2, output_kernel, [((OWN, 256), BF)], [], stream, *down)
    dn, pack, xq, raw = call(
        7,
        functools.partial(qkv_in_place, qkv_back_kernel),
        [((4, OWN, 256), BF), ((8, PACK), F32), ((OWN, 256), F32), ((OWN, 768), BF)],
        [((OWN, 256), F32), ((OWN, 256), F32), ((1, D), F32)],
        place, dq, dk, dv, da_lo, da_hi, qx, kx, vx, cos, sin, xo, stat1, gains, gain2, columns(w0, 0, 768),
    )
    dn = mp_terms(dn)
    packs = [pack, *(mp_turn(pack, s) for s in (1, 2, 3))]
    raw, g1, *rest = lax.optimization_barrier((raw, g1, *dn, *packs))
    dn, packs = rest[:4], rest[4:]
    g1 = scatter_sum(g1, "x")
    (g0,) = call(4, qkv_grads_kernel, [((D, 1152), BF)], [], normed1, raw, go, *packs)
    g0 = sum_of(lax.all_to_all(g0, DP, 0, 0, tiled=True), 32)
    (input_grad,) = call(
        2, leave_kernel, [((OWN, 256), BF)], [],
        place, grad, *dn, *packs, xq, stat1, gains,
    )
    g1 = jnp.where(first, g1[:32], g1[32:]).astype(F32) + turn_by(
        jnp.where(first, g1[32:], g1[:32]), "yh", 1
    ).astype(F32)
    in0, in1, down_t = [
        jnp.concatenate(
            [g1[:, k * MAIN : k * MAIN + MAIN], g1[:, 3 * MAIN + k * TAIL : 3 * MAIN + k * TAIL + TAIL]],
            axis=1,
        )
        for k in range(3)
    ]
    return (
        block_output, input_grad, g0[:, 1024:1026].T[None], g0[:, :768].reshape(1, 32, 3, 256),
        g0[:, 768:1024].T[None], jnp.stack([in0, in1], axis=1)[None], down_t.T[None],
    )


def qkv_in_place(inner, place, dq, dk, dv, *refs):
    *refs, dks, dvs, gsum = refs
    dks[...] = dk[...]
    dvs[...] = dv[...]
    inner(place, dq, dks, dvs, *refs, gsum)


def solution(mesh):
    fine = Mesh(mesh.devices.reshape(4, 4, 2, 2, 2), ("z", "x", "yh", "yl", "c"))
    dp, mp = ("z", "x", "yh"), ("yl", "c")
    return jax.shard_map(
        body,
        mesh=fine,
        in_specs=(
            P(dp, mp),
            P(dp, mp),
            P(None, None, dp),
            P(None, dp, None, mp),
            P(None, mp, dp),
            P(None, dp, None, mp),
            P(None, mp, dp),
        ),
        out_specs=(
            P(dp, mp),
            P(dp, mp),
            P(None, None, dp),
            P(None, dp, None, mp),
            P(None, mp, dp),
            P(None, dp, None, mp),
            P(None, mp, dp),
        ),
        check_vma=False,
    )
```

```python
import functools

import jax
import jax.numpy as jnp
from jax import lax
from jax.experimental import pallas as pl
from jax.experimental.pallas import tpu as pltpu
from jax.sharding import Mesh
from jax.sharding import PartitionSpec as P

HEAD_DIM = 64
REACH = 64
LEN = 2048
EPS = 1e-05
NEG = -1e30
BF = jnp.bfloat16
F32 = jnp.float32
DP = ("z", "x", "yh")

D = 1024
FF = 656
MAIN = 640
TAIL = 16
FFP = 768
VMEM_MB = 62
PACK = 1024 + 384
ROWS = (128, 128, 64, 64)
OWN_AT = (0, 128, 256, 320)
EXT_AT = (0, 256, 512, 704)
OWN = 384
EXT = 896
HALO = 256
NT = (((1,), (1,)), ((), ()))
TN = (((0,), (0,)), ((), ()))


def turn_by(x, axis, by):
    n = lax.axis_size(axis)
    return lax.ppermute(x, axis, [((i + by) % n, i) for i in range(n)])


def sum_of(got, n):
    return jnp.sum(got.reshape(n, got.shape[0] // n, -1).astype(F32), axis=0)


def sum_over(parts, axis):
    n = lax.axis_size(axis)
    total = parts[0].astype(F32)
    for k in range(1, n):
        total = total + lax.ppermute(parts[k], axis, [(i, (i + k) % n) for i in range(n)]).astype(F32)
    return total.astype(BF)


def scatter_sum(x, axis):
    return lax.psum_scatter(x, axis, scatter_dimension=0, tiled=True)


def columns(full, at, width):
    return full, pl.BlockSpec((full.shape[0], width), lambda i: (0, at))


def call(us, body, outs, scratch, *args):
    specs = []
    for a in args:
        if isinstance(a, tuple):
            specs.append(a[1])
        else:
            where = pltpu.SMEM if a.dtype == jnp.int32 else pltpu.VMEM
            specs.append(pl.BlockSpec(memory_space=where))
    return pl.pallas_call(
        body,
        grid=(1,),
        out_shape=[jax.ShapeDtypeStruct(s, t) for s, t in outs],
        in_specs=specs,
        out_specs=[pl.BlockSpec(memory_space=pltpu.VMEM)] * len(outs),
        scratch_shapes=[pltpu.VMEM(s, t) for s, t in scratch],
        cost_estimate=pl.CostEstimate(flops=us * 10**9, bytes_accessed=0, transcendentals=0),
        compiler_params=pltpu.CompilerParams(vmem_limit_bytes=VMEM_MB * 1024 * 1024),
    )(*[a[0] if isinstance(a, tuple) else a for a in args])


def mm(a, b):
    return jnp.dot(a, b, preferred_element_type=F32)


def nt(a, b):
    return lax.dot_general(a, b, NT, preferred_element_type=F32)


def tn(a, b):
    return lax.dot_general(a, b, TN, preferred_element_type=F32)


def block(place, s):
    return pl.ds(pl.multiple_of((place[0] ^ s) * 256, 256), 256)


def enter_kernel(place, x0, x1, x2, x3, xr, own, stats):
    for s in range(4):
        at, x = block(place, s), (x0, x1, x2, x3)[s]
        own[:, at] = x[0:OWN, :]
        for b in range(4):
            e, o, r = EXT_AT[b], OWN_AT[b], ROWS[b]
            xr[e : e + 64, at] = x[OWN + b * 64 : OWN + b * 64 + 64, :]
            xr[e + 64 : e + 64 + r, at] = x[o : o + r, :]
            k = OWN + HALO + b * 64
            xr[e + 64 + r : e + 128 + r, at] = x[k : k + 64, :]

    @pl.loop(0, EXT // 128)
    def _(i):
        rows = pl.ds(pl.multiple_of(i * 128, 128), 128)
        v = xr[rows, :].astype(F32)
        m = jnp.mean(v, axis=1, keepdims=True)
        v = v - m
        r = lax.rsqrt(jnp.mean(v * v, axis=1, keepdims=True) + EPS)
        lane = lax.broadcasted_iota(jnp.int32, (128, 128), 1)
        stats[rows, :] = jnp.where(lane == 0, m, r)


def normalized(x, stats):
    return (x.astype(F32) - stats[:, 0:1]) * stats[:, 1:2]


def own_rows(ref):
    return jnp.concatenate(
        [ref[EXT_AT[b] + REACH : EXT_AT[b] + REACH + ROWS[b], :] for b in range(4)], axis=0
    )


def load_sum(place, half, far, half_c, far_c, full):
    for s in range(4):
        a, b = ((half, far), (half_c, far_c))[s & 1]
        full[:, block(place, s)] = a[s >> 1].astype(F32) + b[1 - (s >> 1)].astype(F32)


def half_turn(v):
    low = (lax.broadcasted_iota(jnp.int32, v.shape, 1) & 63) < 32
    return jnp.where(low, pltpu.roll(v, 96, axis=1), pltpu.roll(v, 32, axis=1))


def window(place, b, times):
    r = ROWS[b]
    i = lax.broadcasted_iota(jnp.int32, (times * r, r + 128), 0) & (r - 1)
    j = lax.broadcasted_iota(jnp.int32, (times * r, r + 128), 1)
    begin = (place[1] * r) & (LEN - 1)
    at = j + (begin - REACH)
    return (j >= i) & (j <= i + 128) & (at >= 0) & (at < LEN)


def head_lanes(shape, h):
    return (lax.broadcasted_iota(jnp.int32, shape, 1) >> 6) == h


def only(v, h):
    return jnp.where(head_lanes(v.shape, h), v, jnp.zeros_like(v))


def by_head(v):
    return jnp.concatenate([only(v, h) for h in range(4)], axis=0)


def join_heads(v, r):
    out = v[0:r]
    for h in range(1, 4):
        out = jnp.where(head_lanes(out.shape, h), v[h * r : h * r + r], out)
    return out


def columns_of(v, first, r):
    return jnp.concatenate([v[:, first + h : first + h + 1] for h in range(4)], axis=0)


def attend_kernel(
    place, xr, stat, w, cos, sin,
    gains, normed, qx, kx, vx, att, lse, even, odd, nb, raw,
):
    gains[...] = w[:, 1024:1152].astype(F32).T[0:8]
    g = gains[0:1]

    @pl.loop(0, EXT // 128)
    def _(i):
        rows = pl.ds(pl.multiple_of(i * 128, 128), 128)
        nb[rows, :] = (normalized(xr[rows, :], stat[rows, :]) * g).astype(BF)

    for b in range(4):
        e, o, r = EXT_AT[b] + REACH, OWN_AT[b], ROWS[b]
        normed[o : o + r, :] = nb[e : e + r, :]
    for t in range(3):
        into = (qx, kx, vx)[t]
        raw[...] = mm(nb[...], w[:, t * 256 : t * 256 + 256])
        for h in range(2):
            lanes = slice(h * 128, h * 128 + 128)
            v = raw[:, lanes]
            if t < 2:
                v = v * cos[...] + half_turn(v) * sin[...]
            into[:, lanes] = v.astype(BF)
    for b in range(4):
        e, at, r = EXT_AT[b], OWN_AT[b], ROWS[b]
        allowed = window(place, b, 4)
        x = nt(by_head(qx[e + 64 : e + 64 + r, :]), kx[e : e + r + 128, :]) * 0.125
        x = jnp.where(allowed, x, NEG)
        most = jnp.max(x, axis=1, keepdims=True)
        x = jnp.exp(x - most)
        total = jnp.sum(x, axis=1, keepdims=True)
        y = mm((x * (1.0 / total)).astype(BF), vx[e : e + r + 128, :])
        att[at : at + r, :] = join_heads(y, r).astype(BF)
        total = most + jnp.log(total)
        lane = lax.broadcasted_iota(jnp.int32, (r, 128), 1)
        kept = jnp.zeros((r, 128), F32)
        for h in range(4):
            kept = jnp.where(lane == h, total[h * r : h * r + r], kept)
        lse[at : at + r, :] = kept
    for s in range(4):
        y = nt(att[...], w[block(place, s), 768:1024])
        (even, odd)[s & 1][s >> 1] = y.astype(BF)


def tail_of(tail, k):
    v = tail.astype(F32)
    v = v if k == 0 else pltpu.roll(v, 128 - k * TAIL, axis=1)
    lane = lax.broadcasted_iota(jnp.int32, v.shape, 1)
    return jnp.where(lane < TAIL, v, 0.0).astype(BF)


def mlp_kernel(
    place, xo, half, far, half_c, far_c, gains, w, c0, c1, c2, c3,
    ct, own, xhat, rinv, normed, act, de0, de1, even, odd, gpart,
    w0, w1, wd, stream,
):
    for s in range(4):
        ct[:, block(place, s)] = (c0, c1, c2, c3)[s][...]
    tail = w[:, 3 * MAIN :]
    for k, full in enumerate((w0, w1, wd)):
        full[:, 0:MAIN] = w[:, k * MAIN : k * MAIN + MAIN]
        full[:, MAIN:] = tail_of(tail, k)

    gain = gains[1:2]
    load_sum(place, half, far, half_c, far_c, stream)
    stream[...] += xo[...].astype(F32)
    own[...] = stream[:, block(place, 0)]

    @pl.loop(0, OWN // 128)
    def _(i):
        rows = pl.ds(pl.multiple_of(i * 128, 128), 128)
        v = stream[rows, :]
        v = v - jnp.mean(v, axis=1, keepdims=True)
        r = lax.rsqrt(jnp.mean(v * v, axis=1, keepdims=True) + EPS)
        v = v * r
        xhat[rows, :] = v
        rinv[rows, :] = jnp.broadcast_to(r, (128, 128))
        normed[rows, :] = (v * gain).astype(BF)

    @pl.loop(0, FFP // 256)
    def _(n):
        at = pl.ds(pl.multiple_of(n * 256, 256), 256)
        e0 = mm(normed[...], w0[:, at])
        e1 = mm(normed[...], w1[:, at])
        da = mm(ct[...], wd[:, at])
        cdf = 0.5 * (1.0 + lax.erf(e0 * 0.7071067811865476))
        pdf = jnp.exp(-0.5 * e0 * e0) * 0.3989422804014327
        ge = e0 * cdf
        act[:, at] = (ge * e1).astype(BF)
        de0[:, at] = (da * e1 * (cdf + e0 * pdf)).astype(BF)
        de1[:, at] = (da * ge).astype(BF)

    for s in range(4):
        at = block(place, s)
        y = nt(de0[...], w0[at, :]) + nt(de1[...], w1[at, :])
        (even, odd)[s & 1][s >> 1] = y.astype(BF)
        gpart[:, at] = jnp.sum(y * xhat[:, at], axis=0, keepdims=True)


def mlp_grads_kernel(place, normed, act, de0, de1, ct, wm, wt, down, g, wd):
    wd[:, 0:MAIN] = wm[...]
    wd[:, MAIN:] = tail_of(wt[...], 2)
    for s in range(4):
        down[s] = nt(act[...], wd[block(place, s), :]).astype(BF)
    lane = lax.broadcasted_iota(jnp.int32, (256, 128), 1)
    for k in range(4):
        at = slice(k * 256, k * 256 + 256)
        n, c = normed[:, at], ct[:, at]
        y0, y1, y2 = tn(n, de0[...]), tn(n, de1[...]), tn(c, act[...])
        tail = jnp.zeros((256, 128), F32)
        for t, y in enumerate((y0, y1, y2)):
            end = jnp.where(lane < TAIL, y[:, MAIN:], 0.0)
            tail = tail + (end if t == 0 else pltpu.roll(end, t * TAIL, axis=1))
        for t, y in enumerate((y0, y1, y2)):
            g[at, t * MAIN : t * MAIN + MAIN] = y[:, 0:MAIN].astype(BF)
        g[at, 3 * MAIN :] = tail.astype(BF)


def edges(ref, last):
    at = [OWN_AT[b] + (ROWS[b] - 64 if last else 0) for b in range(4)]
    return jnp.concatenate([ref[k : k + 64, :] for k in at], axis=0)


def norm_back_kernel(
    place, half, far, half_c, far_c, ct, xhat, rinv, gains, w, att, lse,
    own, gb, da, da_first, da_last,
    grad, stat,
):
    gain = gains[1:2]
    load_sum(place, half, far, half_c, far_c, grad)

    @pl.loop(0, OWN // 128)
    def _(i):
        rows = pl.ds(pl.multiple_of(i * 128, 128), 128)
        e = grad[rows, :] * gain
        x = xhat[rows, :]
        m1 = jnp.mean(e, axis=1, keepdims=True)
        m2 = jnp.mean(e * x, axis=1, keepdims=True)
        r = rinv[rows, 0:1]
        g = ct[rows, :].astype(F32) + r * (e - m1 - x * m2)
        grad[rows, :] = g
        gb[rows, :] = g.astype(BF)

    own[...] = grad[:, block(place, 0)]
    da[...] = mm(gb[...], w[...]).astype(BF)
    prod = da[...].astype(F32) * att[...].astype(F32)
    lane = lax.broadcasted_iota(jnp.int32, (OWN, 128), 1)
    kept = lse[...]
    for h in range(4):
        centre = jnp.sum(only(prod, h), axis=1, keepdims=True)
        kept = jnp.where(lane == 4 + h, centre, kept)
    stat[...] = kept
    for out, last in ((da_first, False), (da_last, True)):
        out[0:HALO, :] = edges(da, last)
        st = edges(stat, last).T[0:8]
        high = st.astype(BF)
        rest = (st - high.astype(F32)).astype(BF)
        out[HALO : HALO + 16, :] = jnp.concatenate([high.astype(F32), rest.astype(F32)], axis=0).astype(BF)


def attend_back_kernel(place, da, lse, gb, att, qx, kx, vx, go, dq, dk, dv):
    for b in range(4):
        e, o, r = EXT_AT[b], OWN_AT[b], ROWS[b]
        q, d = by_head(qx[e + 64 : e + 64 + r, :]), by_head(da[o : o + r, :])
        k, v = kx[e : e + r + 128, :], vx[e : e + r + 128, :]
        total = columns_of(lse[o : o + r, :], 0, r)
        p = jnp.exp(jnp.where(window(place, b, 4), nt(q, k) * 0.125 - total, NEG))
        dp = nt(d, v)
        ds = (p * (dp - jnp.sum(p * dp, axis=1, keepdims=True))).astype(BF)
        dq[o : o + r, :] = join_heads(mm(ds, k), r) * 0.125
        dk[o : o + r, :] = tn(ds, q)[64 : 64 + r] * 0.125
        dv[o : o + r, :] = tn(p.astype(BF), d)[64 : 64 + r]
    for k in range(4):
        go[k * 256 : k * 256 + 256, :] = tn(gb[:, k * 256 : k * 256 + 256], att[...]).astype(BF)


def qkv_back_kernel(
    place, dq, dk, dv, da_lo, da_hi, qx, kx, vx, cos, sin, xo, stat, gains, gain2, w,
    even, odd, pack, xq, raw, gsum,
):
    i = lax.broadcasted_iota(jnp.int32, (256, 64), 0) & 63
    j = lax.broadcasted_iota(jnp.int32, (256, 64), 1)
    pad = jnp.zeros((120, HALO), F32)
    known = []
    for ref in (da_lo, da_hi):
        st = ref[HALO : HALO + 16, :].astype(F32)
        known.append(jnp.concatenate([st[0:8] + st[8:16], pad], axis=0).T)
    for b in range(4):
        e, o, r = EXT_AT[b], OWN_AT[b], ROWS[b]
        begin = (place[1] * r) & (LEN - 1)
        at = slice(b * 64, b * 64 + 64)
        for side in range(2):
            of = e if side == 0 else e + 64 + r
            keys = e + 64 if side == 0 else e + r
            to = slice(o, o + 64) if side == 0 else slice(o + r - 64, o + r)
            allowed = (j <= i) & (begin != 0) if side == 0 else (j >= i) & (begin + r != LEN)
            q, d = by_head(qx[of : of + 64, :]), by_head((da_lo, da_hi)[side][at, :])
            k, v = kx[keys : keys + 64, :], vx[keys : keys + 64, :]
            st = known[side][at]
            p = jnp.exp(jnp.where(allowed, nt(q, k) * 0.125 - columns_of(st, 0, 64), NEG))
            ds = (p * (nt(d, v) - columns_of(st, 4, 64))).astype(BF)
            dk[to, :] += tn(ds, q) * 0.125
            dv[to, :] += tn(p.astype(BF), d)
    for b in range(4):
        e, o, r = EXT_AT[b] + REACH, OWN_AT[b], ROWS[b]
        c, s = cos[e : e + r, :], sin[e : e + r, :]
        for t in range(2):
            lanes = slice(t * 128, t * 128 + 128)
            v = dq[o : o + r, lanes]
            raw[o : o + r, lanes] = (v * c - half_turn(v) * s).astype(BF)
            v = dk[o : o + r, lanes]
            lanes = slice(256 + t * 128, 256 + t * 128 + 128)
            raw[o : o + r, lanes] = (v * c - half_turn(v) * s).astype(BF)
    raw[:, 512:768] = dv[...].astype(BF)
    st = own_rows(stat)
    m1 = jnp.zeros((OWN, 1), F32)
    m2 = jnp.zeros((OWN, 1), F32)
    for s in range(4):
        at = block(place, s)
        y = nt(raw[...], w[at, :])
        (even, odd)[s & 1][s >> 1] = y.astype(BF)
        x = normalized(xo[:, at], st)
        if s == 0:
            xq[...] = x
        e = y * gains[0:1, at]
        m1 = m1 + jnp.sum(e, axis=1, keepdims=True)
        m2 = m2 + jnp.sum(e * x, axis=1, keepdims=True)
        gsum[:, at] = jnp.sum(y * x, axis=0, keepdims=True)
    lane = lax.broadcasted_iota(jnp.int32, (OWN, 128), 1)
    sums = jnp.where(lane == 0, m1, jnp.where(lane == 1, m2, 0.0)) * (1.0 / D)
    pack[:, D:] = sums.T[0:8]
    pack[0:1, 0:D] = gsum[...]
    pack[1:2, 0:D] = gain2[...]


def qkv_grads_kernel(normed, raw, go, g):
    for k in range(4):
        at = slice(k * 256, k * 256 + 256)
        g[at, 0:768] = tn(normed[:, at], raw[...]).astype(BF)
    g[:, 768:1024] = go[...]


def gain_columns_kernel(p0, p1, p2, p3, g, out):
    row = lax.broadcasted_iota(jnp.int32, (8, D), 0)
    both = jnp.where(row < 2, p0[:, :D] + p1[:, :D] + p2[:, :D] + p3[:, :D], 0.0)
    out[...] = jnp.concatenate([both, jnp.zeros((120, D), F32)], axis=0).T.astype(BF)


def with_gains(g, packs):
    return pl.pallas_call(
        gain_columns_kernel,
        grid=(1,),
        out_shape=jax.ShapeDtypeStruct(g.shape, g.dtype),
        in_specs=[pl.BlockSpec(memory_space=pltpu.VMEM)] * 4 + [pl.BlockSpec(memory_space=pl.ANY)],
        out_specs=pl.BlockSpec((D, 128), lambda i: (0, 8)),
        input_output_aliases={4: 0},
        cost_estimate=pl.CostEstimate(flops=10**9, bytes_accessed=0, transcendentals=0),
        compiler_params=pltpu.CompilerParams(vmem_limit_bytes=VMEM_MB * 1024 * 1024),
    )(*packs, g)


def leave_kernel(place, grad, own, a, p0, p1, p2, p3, xq, stat, gains, out):
    sums = p0[:, D:] + p1[:, D:] + p2[:, D:] + p3[:, D:]
    sums = jnp.concatenate([sums, jnp.zeros((120, OWN), F32)], axis=0).T
    m1, m2 = sums[:, 0:1], sums[:, 1:2]
    e = own[0].astype(F32) + a[...].astype(F32)
    e = e * gains[0:1, block(place, 0)]
    y = grad[...] + own_rows(stat)[:, 1:2] * (e - m1 - xq[...] * m2)
    out[...] = y.astype(BF)


def output_kernel(stream, own, a, b, c, out):
    y = stream[...] + own[0].astype(F32) + a[...].astype(F32)
    out[...] = (y + b[...].astype(F32) + c[...].astype(F32)).astype(BF)


def mp_gather(x):
    far = turn_by(x, "yl", 1)
    return x, turn_by(x, "c", 1), far, turn_by(far, "c", 1)


def mp_turn(x, slot):
    return lax.ppermute(x, ("yl", "c"), [(i, i ^ slot) for i in range(4)])


def mp_terms(slots):
    return [slots, *(mp_turn(slots[s], s) for s in (1, 2, 3))]


def mp_reduce(even, odd):
    return (even.astype(F32) + turn_by(odd, "c", 1).astype(F32)).astype(BF)


def mp_sum(even, odd):
    half = mp_reduce(even, odd)
    far = turn_by(half, "yl", 1)
    return half, far, turn_by(half, "c", 1), turn_by(far, "c", 1)


def dp_turn(x, by):
    pairs = [(i, i + by) for i in range(32) if 0 <= i + by < 32]
    return lax.ppermute(x, ("z", "x", "yh"), pairs)


def rope_tables(place):
    rows = []
    for b in range(4):
        r = ROWS[b]
        rows.append((place * r + jnp.arange(r + 128, dtype=jnp.int32) - REACH) % LEN)
    position = jnp.concatenate(rows).astype(F32)
    frequency = 1.0 / 10000.0 ** (jnp.arange(0, HEAD_DIM, 2, dtype=F32) / HEAD_DIM)
    angles = position[:, None] * frequency[None, :]
    c, s = jnp.cos(angles), jnp.sin(angles)
    return jnp.concatenate([c, c, c, c], axis=1), jnp.concatenate([-s, s, -s, s], axis=1)


def body(block_input, cotangent, norm_gain, w_qkv, w_out, w_in, w_down):
    mp = lax.axis_index("yl") * 2 + lax.axis_index("c")
    dp = (lax.axis_index("z") * 4 + lax.axis_index("x")) * 2 + lax.axis_index("yh")
    place = jnp.stack([mp, dp]).astype(jnp.int32)

    gain_t = jnp.pad(norm_gain[0].T, ((0, 0), (0, 126)))
    shard0 = jnp.concatenate([w_qkv[0].reshape(32, 768), w_out[0].T, gain_t], axis=1)
    in0, in1, down_t = w_in[0, :, 0], w_in[0, :, 1], w_down[0].T
    shard1 = jnp.concatenate(
        [in0[:, :MAIN], in1[:, :MAIN], down_t[:, :MAIN]]
        + [in0[:, MAIN:], in1[:, MAIN:], down_t[:, MAIN:], jnp.zeros((32, 128 - 3 * TAIL), BF)],
        axis=1,
    )
    shard = jnp.concatenate([shard0, shard1], axis=1)
    lows = jnp.concatenate([block_input[o + r - 64 : o + r] for o, r in zip(OWN_AT, ROWS)], axis=0)
    highs = jnp.concatenate([block_input[o : o + 64] for o in OWN_AT], axis=0)
    lows, highs, shard = lax.optimization_barrier((lows, highs, shard))
    low, high = dp_turn(lows, 1), dp_turn(highs, -1)
    pair = turn_by(shard, "yh", 1)
    low, high, pair = lax.optimization_barrier((low, high, pair))
    first = lax.axis_index("yh") == 0
    pair = [jnp.where(first, shard, pair), jnp.where(first, pair, shard)]
    pair = jnp.concatenate(pair, axis=0)
    spread = jnp.broadcast_to(pair[None, :, :1152], (16, 64, 1152)).reshape(D, 1152)
    w0 = lax.all_to_all(spread, ("z", "x"), 0, 0, tiled=True)
    w1 = lax.all_gather(pair[:, 1152:], ("z", "x"), axis=0, tiled=True)
    x_slots = mp_gather(jnp.concatenate([block_input, low, high], axis=0))
    cos, sin = rope_tables(dp)

    xr, xo, stat1 = call(
        5, enter_kernel, [((EXT, D), BF), ((OWN, D), BF), ((EXT, 128), F32)], [], place, *x_slots
    )
    xr, cotangent = lax.optimization_barrier((xr, cotangent))
    xr, *c_slots = lax.optimization_barrier((xr, *mp_gather(cotangent)))
    slots = [((2, OWN, 256), BF)] * 2
    gains, normed1, qx, kx, vx, att, lse, *parts = call(
        10,
        attend_kernel,
        [((8, D), F32), ((OWN, D), BF), ((EXT, 256), BF), ((EXT, 256), BF), ((EXT, 256), BF)]
        + [((OWN, 256), BF), ((OWN, 128), F32)] + slots,
        [((EXT, D), BF), ((EXT, 256), F32)],
        place, xr, stat1, w0, cos, sin,
    )
    ct, stream, xhat2, rinv2, normed2, act, de0, de1, even, odd, gain2 = call(
        10,
        mlp_kernel,
        [
            ((OWN, D), BF), ((OWN, 256), F32), ((OWN, D), F32), ((OWN, 128), F32), ((OWN, D), BF),
            ((OWN, FFP), BF), ((OWN, FFP), BF), ((OWN, FFP), BF),
            *slots, ((1, D), F32),
        ],
        [((D, FFP), BF), ((D, FFP), BF), ((D, FFP), BF), ((OWN, D), F32)],
        place, xo, *mp_sum(*parts), gains, w1, *c_slots,
    )
    half = mp_reduce(even, odd)
    far = turn_by(half, "yl", 1)
    half_c = turn_by(half, "c", 1)
    down, g1 = call(
        9,
        mlp_grads_kernel,
        [((4, OWN, 256), BF), ((D, 2048), BF)],
        [((D, FFP), BF)],
        place, normed2, act, de0, de1, ct, columns(w1, 2, MAIN), columns(w1, 15, 128),
    )
    far, down, g1 = lax.optimization_barrier((far, down, g1))
    far_c = turn_by(far, "c", 1)
    g1 = scatter_sum(g1, "z")
    down = mp_terms(down)

    grad, gb, da, da_first, da_last = call(
        6,
        norm_back_kernel,
        [((OWN, 256), F32), ((OWN, D), BF), ((OWN, 256), BF)]
        + [((HALO + 16, 256), BF)] * 2,
        [((OWN, D), F32), ((OWN, 128), F32)],
        place, half, far, half_c, far_c, ct, xhat2, rinv2, gains, columns(w0, 3, 256), att, lse,
    )
    gb, *down = lax.optimization_barrier((gb, *down))
    da_lo, da_hi = dp_turn(da_last, 1), dp_turn(da_first, -1)
    go, dq, dk, dv = call(
        8,
        attend_back_kernel,
        [((D, 256), BF)] + [((OWN, 256), F32)] * 3,
        [],
        place, da, lse, gb, att, qx, kx, vx,
    )
    even, odd, pack, xq, raw = call(
        7,
        functools.partial(qkv_in_place, qkv_back_kernel),
        [*slots, ((8, PACK), F32), ((OWN, 256), F32), ((OWN, 768), BF)],
        [((OWN, 256), F32), ((OWN, 256), F32), ((1, D), F32)],
        place, dq, dk, dv, da_lo, da_hi, qx, kx, vx, cos, sin, xo, stat1, gains, gain2, columns(w0, 0, 768),
    )
    half = mp_reduce(even, odd)
    half, normed1 = lax.optimization_barrier((half, normed1))
    dn = [half, turn_by(half[1], "yl", 1)]
    packs = [pack, *(mp_turn(pack, s) for s in (1, 2, 3))]
    (g0,) = call(4, qkv_grads_kernel, [((D, 1152), BF)], [], normed1, raw, go)
    at = lax.axis_index("x")
    parts = [lax.dynamic_slice_in_dim(g1, ((at + k) % 4) * 64, 64, 0) for k in range(4)]
    g0, *rest = lax.optimization_barrier((g0, *dn, *packs, *parts))
    dn, packs, parts = rest[:2], rest[2:6], rest[6:]
    g1 = sum_over(parts, "x")
    g0 = with_gains(g0, packs)
    g0, *down = lax.optimization_barrier((g0, *down))
    (block_output,) = call(2, output_kernel, [((OWN, 256), BF)], [], stream, *down)
    g0 = sum_of(lax.all_to_all(g0, DP, 0, 0, tiled=True), 32)
    (input_grad,) = call(
        2, leave_kernel, [((OWN, 256), BF)], [],
        place, grad, *dn, *packs, xq, stat1, gains,
    )
    g1 = jnp.where(first, g1[:32], g1[32:]).astype(F32) + turn_by(
        jnp.where(first, g1[32:], g1[:32]), "yh", 1
    ).astype(F32)
    in0, in1, down_t = [
        jnp.concatenate(
            [g1[:, k * MAIN : k * MAIN + MAIN], g1[:, 3 * MAIN + k * TAIL : 3 * MAIN + k * TAIL + TAIL]],
            axis=1,
        )
        for k in range(3)
    ]
    return (
        block_output, input_grad, g0[:, 1024:1026].T[None], g0[:, :768].reshape(1, 32, 3, 256),
        g0[:, 768:1024].T[None], jnp.stack([in0, in1], axis=1)[None], down_t.T[None],
    )


def qkv_in_place(inner, place, dq, dk, dv, *refs):
    *refs, dks, dvs, gsum = refs
    dks[...] = dk[...]
    dvs[...] = dv[...]
    inner(place, dq, dks, dvs, *refs, gsum)


def solution(mesh):
    fine = Mesh(mesh.devices.reshape(4, 4, 2, 2, 2), ("z", "x", "yh", "yl", "c"))
    dp, mp = ("z", "x", "yh"), ("yl", "c")
    return jax.shard_map(
        body,
        mesh=fine,
        in_specs=(
            P(dp, mp),
            P(dp, mp),
            P(None, None, dp),
            P(None, dp, None, mp),
            P(None, mp, dp),
            P(None, dp, None, mp),
            P(None, mp, dp),
        ),
        out_specs=(
            P(dp, mp),
            P(dp, mp),
            P(None, None, dp),
            P(None, dp, None, mp),
            P(None, mp, dp),
            P(None, dp, None, mp),
            P(None, mp, dp),
        ),
        check_vma=False,
    )
```

```python
import functools

import jax
import jax.numpy as jnp
from jax import lax
from jax.experimental import pallas as pl
from jax.experimental.pallas import tpu as pltpu
from jax.sharding import Mesh
from jax.sharding import PartitionSpec as P

HEAD_DIM = 64
REACH = 64
LEN = 2048
EPS = 1e-05
NEG = -1e30
BF = jnp.bfloat16
F32 = jnp.float32
DP = ("z", "x", "yh")

D = 1024
FF = 656
MAIN = 640
TAIL = 16
FFP = 768
VMEM_MB = 62
PACK = 1024 + 384
ROWS = (128, 128, 64, 64)
OWN_AT = (0, 128, 256, 320)
EXT_AT = (0, 256, 512, 704)
OWN = 384
EXT = 896
HALO = 256
NT = (((1,), (1,)), ((), ()))
TN = (((0,), (0,)), ((), ()))


def turn_by(x, axis, by):
    n = lax.axis_size(axis)
    return lax.ppermute(x, axis, [((i + by) % n, i) for i in range(n)])


def sum_of(got, n):
    return jnp.sum(got.reshape(n, got.shape[0] // n, -1).astype(F32), axis=0)


def sum_over(parts, axis):
    n = lax.axis_size(axis)
    total = parts[0].astype(F32)
    for k in range(1, n):
        total = total + lax.ppermute(parts[k], axis, [(i, (i + k) % n) for i in range(n)]).astype(F32)
    return total.astype(BF)


def scatter_sum(x, axis):
    return lax.psum_scatter(x, axis, scatter_dimension=0, tiled=True)


def columns(full, at, width):
    return full, pl.BlockSpec((full.shape[0], width), lambda i: (0, at))


def call(us, body, outs, scratch, *args):
    specs = []
    for a in args:
        if isinstance(a, tuple):
            specs.append(a[1])
        else:
            where = pltpu.SMEM if a.dtype == jnp.int32 else pltpu.VMEM
            specs.append(pl.BlockSpec(memory_space=where))
    return pl.pallas_call(
        body,
        grid=(1,),
        out_shape=[jax.ShapeDtypeStruct(s, t) for s, t in outs],
        in_specs=specs,
        out_specs=[pl.BlockSpec(memory_space=pltpu.VMEM)] * len(outs),
        scratch_shapes=[pltpu.VMEM(s, t) for s, t in scratch],
        cost_estimate=pl.CostEstimate(flops=us * 10**9, bytes_accessed=0, transcendentals=0),
        compiler_params=pltpu.CompilerParams(vmem_limit_bytes=VMEM_MB * 1024 * 1024),
    )(*[a[0] if isinstance(a, tuple) else a for a in args])


def mm(a, b):
    return jnp.dot(a, b, preferred_element_type=F32)


def nt(a, b):
    return lax.dot_general(a, b, NT, preferred_element_type=F32)


def tn(a, b):
    return lax.dot_general(a, b, TN, preferred_element_type=F32)


def block(place, s):
    return pl.ds(pl.multiple_of((place[0] ^ s) * 256, 256), 256)


def enter_kernel(place, x0, x1, x2, x3, xr, own, stats):
    for s in range(4):
        at, x = block(place, s), (x0, x1, x2, x3)[s]
        own[:, at] = x[0:OWN, :]
        for b in range(4):
            e, o, r = EXT_AT[b], OWN_AT[b], ROWS[b]
            xr[e : e + 64, at] = x[OWN + b * 64 : OWN + b * 64 + 64, :]
            xr[e + 64 : e + 64 + r, at] = x[o : o + r, :]
            k = OWN + HALO + b * 64
            xr[e + 64 + r : e + 128 + r, at] = x[k : k + 64, :]

    @pl.loop(0, EXT // 128)
    def _(i):
        rows = pl.ds(pl.multiple_of(i * 128, 128), 128)
        v = xr[rows, :].astype(F32)
        m = jnp.mean(v, axis=1, keepdims=True)
        v = v - m
        r = lax.rsqrt(jnp.mean(v * v, axis=1, keepdims=True) + EPS)
        lane = lax.broadcasted_iota(jnp.int32, (128, 128), 1)
        stats[rows, :] = jnp.where(lane == 0, m, r)


def normalized(x, stats):
    return (x.astype(F32) - stats[:, 0:1]) * stats[:, 1:2]


def own_rows(ref):
    return jnp.concatenate(
        [ref[EXT_AT[b] + REACH : EXT_AT[b] + REACH + ROWS[b], :] for b in range(4)], axis=0
    )


def load_sum(place, half, far, half_c, far_c, full):
    for s in range(4):
        a, b = ((half, far), (half_c, far_c))[s & 1]
        full[:, block(place, s)] = a[s >> 1].astype(F32) + b[1 - (s >> 1)].astype(F32)


def half_turn(v):
    low = (lax.broadcasted_iota(jnp.int32, v.shape, 1) & 63) < 32
    return jnp.where(low, pltpu.roll(v, 96, axis=1), pltpu.roll(v, 32, axis=1))


def window(place, b, times):
    r = ROWS[b]
    i = lax.broadcasted_iota(jnp.int32, (times * r, r + 128), 0) & (r - 1)
    j = lax.broadcasted_iota(jnp.int32, (times * r, r + 128), 1)
    begin = (place[1] * r) & (LEN - 1)
    at = j + (begin - REACH)
    return (j >= i) & (j <= i + 128) & (at >= 0) & (at < LEN)


def head_lanes(shape, h):
    return (lax.broadcasted_iota(jnp.int32, shape, 1) >> 6) == h


def only(v, h):
    return jnp.where(head_lanes(v.shape, h), v, jnp.zeros_like(v))


def by_head(v):
    return jnp.concatenate([only(v, h) for h in range(4)], axis=0)


def join_heads(v, r):
    out = v[0:r]
    for h in range(1, 4):
        out = jnp.where(head_lanes(out.shape, h), v[h * r : h * r + r], out)
    return out


def columns_of(v, first, r):
    return jnp.concatenate([v[:, first + h : first + h + 1] for h in range(4)], axis=0)


def attend_kernel(
    place, xr, stat, w, cos, sin,
    gains, normed, qx, kx, vx, att, lse, even, odd, nb, raw,
):
    gains[...] = w[:, 1024:1152].astype(F32).T[0:8]
    g = gains[0:1]

    @pl.loop(0, EXT // 128)
    def _(i):
        rows = pl.ds(pl.multiple_of(i * 128, 128), 128)
        nb[rows, :] = (normalized(xr[rows, :], stat[rows, :]) * g).astype(BF)

    for b in range(4):
        e, o, r = EXT_AT[b] + REACH, OWN_AT[b], ROWS[b]
        normed[o : o + r, :] = nb[e : e + r, :]
    for t in range(3):
        into = (qx, kx, vx)[t]
        raw[...] = mm(nb[...], w[:, t * 256 : t * 256 + 256])
        for h in range(2):
            lanes = slice(h * 128, h * 128 + 128)
            v = raw[:, lanes]
            if t < 2:
                v = v * cos[...] + half_turn(v) * sin[...]
            into[:, lanes] = v.astype(BF)
    for b in range(4):
        e, at, r = EXT_AT[b], OWN_AT[b], ROWS[b]
        allowed = window(place, b, 4)
        x = nt(by_head(qx[e + 64 : e + 64 + r, :]), kx[e : e + r + 128, :]) * 0.125
        x = jnp.where(allowed, x, NEG)
        most = jnp.max(x, axis=1, keepdims=True)
        x = jnp.exp(x - most)
        total = jnp.sum(x, axis=1, keepdims=True)
        y = mm((x * (1.0 / total)).astype(BF), vx[e : e + r + 128, :])
        att[at : at + r, :] = join_heads(y, r).astype(BF)
        total = most + jnp.log(total)
        lane = lax.broadcasted_iota(jnp.int32, (r, 128), 1)
        kept = jnp.zeros((r, 128), F32)
        for h in range(4):
            kept = jnp.where(lane == h, total[h * r : h * r + r], kept)
        lse[at : at + r, :] = kept
    for s in range(4):
        y = nt(att[...], w[block(place, s), 768:1024])
        (even, odd)[s & 1][s >> 1] = y.astype(BF)


def tail_of(tail, k):
    v = tail.astype(F32)
    v = v if k == 0 else pltpu.roll(v, 128 - k * TAIL, axis=1)
    lane = lax.broadcasted_iota(jnp.int32, v.shape, 1)
    return jnp.where(lane < TAIL, v, 0.0).astype(BF)


def mlp_kernel(
    place, xo, half, far, half_c, far_c, gains, w, c0, c1, c2, c3,
    ct, own, xhat, rinv, normed, act, de0, de1, even, odd, gpart,
    w0, w1, wd, stream,
):
    for s in range(4):
        ct[:, block(place, s)] = (c0, c1, c2, c3)[s][...]
    tail = w[:, 3 * MAIN :]
    for k, full in enumerate((w0, w1, wd)):
        full[:, 0:MAIN] = w[:, k * MAIN : k * MAIN + MAIN]
        full[:, MAIN:] = tail_of(tail, k)

    gain = gains[1:2]
    load_sum(place, half, far, half_c, far_c, stream)
    stream[...] += xo[...].astype(F32)
    own[...] = stream[:, block(place, 0)]

    @pl.loop(0, OWN // 128)
    def _(i):
        rows = pl.ds(pl.multiple_of(i * 128, 128), 128)
        v = stream[rows, :]
        v = v - jnp.mean(v, axis=1, keepdims=True)
        r = lax.rsqrt(jnp.mean(v * v, axis=1, keepdims=True) + EPS)
        v = v * r
        xhat[rows, :] = v
        rinv[rows, :] = jnp.broadcast_to(r, (128, 128))
        normed[rows, :] = (v * gain).astype(BF)

    @pl.loop(0, FFP // 256)
    def _(n):
        at = pl.ds(pl.multiple_of(n * 256, 256), 256)
        e0 = mm(normed[...], w0[:, at])
        e1 = mm(normed[...], w1[:, at])
        da = mm(ct[...], wd[:, at])
        cdf = 0.5 * (1.0 + lax.erf(e0 * 0.7071067811865476))
        pdf = jnp.exp(-0.5 * e0 * e0) * 0.3989422804014327
        ge = e0 * cdf
        act[:, at] = (ge * e1).astype(BF)
        de0[:, at] = (da * e1 * (cdf + e0 * pdf)).astype(BF)
        de1[:, at] = (da * ge).astype(BF)

    for s in range(4):
        at = block(place, s)
        y = nt(de0[...], w0[at, :]) + nt(de1[...], w1[at, :])
        (even, odd)[s & 1][s >> 1] = y.astype(BF)
        gpart[:, at] = jnp.sum(y * xhat[:, at], axis=0, keepdims=True)


def mlp_grads_kernel(place, normed, act, de0, de1, ct, wm, wt, down, g, wd):
    wd[:, 0:MAIN] = wm[...]
    wd[:, MAIN:] = tail_of(wt[...], 2)
    for s in range(4):
        down[s] = nt(act[...], wd[block(place, s), :]).astype(BF)
    lane = lax.broadcasted_iota(jnp.int32, (256, 128), 1)
    for k in range(4):
        at = slice(k * 256, k * 256 + 256)
        n, c = normed[:, at], ct[:, at]
        y0, y1, y2 = tn(n, de0[...]), tn(n, de1[...]), tn(c, act[...])
        tail = jnp.zeros((256, 128), F32)
        for t, y in enumerate((y0, y1, y2)):
            end = jnp.where(lane < TAIL, y[:, MAIN:], 0.0)
            tail = tail + (end if t == 0 else pltpu.roll(end, t * TAIL, axis=1))
        for t, y in enumerate((y0, y1, y2)):
            g[at, t * MAIN : t * MAIN + MAIN] = y[:, 0:MAIN].astype(BF)
        g[at, 3 * MAIN :] = tail.astype(BF)


def edges(ref, last):
    at = [OWN_AT[b] + (ROWS[b] - 64 if last else 0) for b in range(4)]
    return jnp.concatenate([ref[k : k + 64, :] for k in at], axis=0)


def norm_back_kernel(
    place, half, far, half_c, far_c, ct, xhat, rinv, gains, w, att, lse,
    own, gb, da, da_first, da_last,
    grad, stat,
):
    gain = gains[1:2]
    load_sum(place, half, far, half_c, far_c, grad)

    @pl.loop(0, OWN // 128)
    def _(i):
        rows = pl.ds(pl.multiple_of(i * 128, 128), 128)
        e = grad[rows, :] * gain
        x = xhat[rows, :]
        m1 = jnp.mean(e, axis=1, keepdims=True)
        m2 = jnp.mean(e * x, axis=1, keepdims=True)
        r = rinv[rows, 0:1]
        g = ct[rows, :].astype(F32) + r * (e - m1 - x * m2)
        grad[rows, :] = g
        gb[rows, :] = g.astype(BF)

    own[...] = grad[:, block(place, 0)]
    da[...] = mm(gb[...], w[...]).astype(BF)
    prod = da[...].astype(F32) * att[...].astype(F32)
    lane = lax.broadcasted_iota(jnp.int32, (OWN, 128), 1)
    kept = lse[...]
    for h in range(4):
        centre = jnp.sum(only(prod, h), axis=1, keepdims=True)
        kept = jnp.where(lane == 4 + h, centre, kept)
    stat[...] = kept
    for out, last in ((da_first, False), (da_last, True)):
        out[0:HALO, :] = edges(da, last)
        st = edges(stat, last).T[0:8]
        high = st.astype(BF)
        rest = (st - high.astype(F32)).astype(BF)
        out[HALO : HALO + 16, :] = jnp.concatenate([high.astype(F32), rest.astype(F32)], axis=0).astype(BF)


def attend_back_kernel(place, da, lse, gb, att, qx, kx, vx, go, dq, dk, dv):
    for b in range(4):
        e, o, r = EXT_AT[b], OWN_AT[b], ROWS[b]
        q, d = by_head(qx[e + 64 : e + 64 + r, :]), by_head(da[o : o + r, :])
        k, v = kx[e : e + r + 128, :], vx[e : e + r + 128, :]
        total = columns_of(lse[o : o + r, :], 0, r)
        p = jnp.exp(jnp.where(window(place, b, 4), nt(q, k) * 0.125 - total, NEG))
        dp = nt(d, v)
        ds = (p * (dp - jnp.sum(p * dp, axis=1, keepdims=True))).astype(BF)
        dq[o : o + r, :] = join_heads(mm(ds, k), r) * 0.125
        dk[o : o + r, :] = tn(ds, q)[64 : 64 + r] * 0.125
        dv[o : o + r, :] = tn(p.astype(BF), d)[64 : 64 + r]
    for k in range(4):
        go[k * 256 : k * 256 + 256, :] = tn(gb[:, k * 256 : k * 256 + 256], att[...]).astype(BF)


def qkv_back_kernel(
    place, dq, dk, dv, da_lo, da_hi, qx, kx, vx, cos, sin, xo, stat, gains, gain2, w,
    even, odd, pack, xq, raw, gsum,
):
    i = lax.broadcasted_iota(jnp.int32, (256, 64), 0) & 63
    j = lax.broadcasted_iota(jnp.int32, (256, 64), 1)
    pad = jnp.zeros((120, HALO), F32)
    known = []
    for ref in (da_lo, da_hi):
        st = ref[HALO : HALO + 16, :].astype(F32)
        known.append(jnp.concatenate([st[0:8] + st[8:16], pad], axis=0).T)
    for b in range(4):
        e, o, r = EXT_AT[b], OWN_AT[b], ROWS[b]
        begin = (place[1] * r) & (LEN - 1)
        at = slice(b * 64, b * 64 + 64)
        for side in range(2):
            of = e if side == 0 else e + 64 + r
            keys = e + 64 if side == 0 else e + r
            to = slice(o, o + 64) if side == 0 else slice(o + r - 64, o + r)
            allowed = (j <= i) & (begin != 0) if side == 0 else (j >= i) & (begin + r != LEN)
            q, d = by_head(qx[of : of + 64, :]), by_head((da_lo, da_hi)[side][at, :])
            k, v = kx[keys : keys + 64, :], vx[keys : keys + 64, :]
            st = known[side][at]
            p = jnp.exp(jnp.where(allowed, nt(q, k) * 0.125 - columns_of(st, 0, 64), NEG))
            ds = (p * (nt(d, v) - columns_of(st, 4, 64))).astype(BF)
            dk[to, :] += tn(ds, q) * 0.125
            dv[to, :] += tn(p.astype(BF), d)
    for b in range(4):
        e, o, r = EXT_AT[b] + REACH, OWN_AT[b], ROWS[b]
        c, s = cos[e : e + r, :], sin[e : e + r, :]
        for t in range(2):
            lanes = slice(t * 128, t * 128 + 128)
            v = dq[o : o + r, lanes]
            raw[o : o + r, lanes] = (v * c - half_turn(v) * s).astype(BF)
            v = dk[o : o + r, lanes]
            lanes = slice(256 + t * 128, 256 + t * 128 + 128)
            raw[o : o + r, lanes] = (v * c - half_turn(v) * s).astype(BF)
    raw[:, 512:768] = dv[...].astype(BF)
    st = own_rows(stat)
    m1 = jnp.zeros((OWN, 1), F32)
    m2 = jnp.zeros((OWN, 1), F32)
    for s in range(4):
        at = block(place, s)
        y = nt(raw[...], w[at, :])
        (even, odd)[s & 1][s >> 1] = y.astype(BF)
        x = normalized(xo[:, at], st)
        if s == 0:
            xq[...] = x
        e = y * gains[0:1, at]
        m1 = m1 + jnp.sum(e, axis=1, keepdims=True)
        m2 = m2 + jnp.sum(e * x, axis=1, keepdims=True)
        gsum[:, at] = jnp.sum(y * x, axis=0, keepdims=True)
    lane = lax.broadcasted_iota(jnp.int32, (OWN, 128), 1)
    sums = jnp.where(lane == 0, m1, jnp.where(lane == 1, m2, 0.0)) * (1.0 / D)
    pack[:, D:] = sums.T[0:8]
    pack[0:1, 0:D] = gsum[...]
    pack[1:2, 0:D] = gain2[...]


def qkv_grads_kernel(normed, raw, go, g):
    for k in range(4):
        at = slice(k * 256, k * 256 + 256)
        g[at, 0:768] = tn(normed[:, at], raw[...]).astype(BF)
    g[:, 768:1024] = go[...]


def gain_columns_kernel(p0, p1, p2, p3, g, out):
    row = lax.broadcasted_iota(jnp.int32, (8, D), 0)
    both = jnp.where(row < 2, p0[:, :D] + p1[:, :D] + p2[:, :D] + p3[:, :D], 0.0)
    out[...] = jnp.concatenate([both, jnp.zeros((120, D), F32)], axis=0).T.astype(BF)


def with_gains(g, packs):
    return pl.pallas_call(
        gain_columns_kernel,
        grid=(1,),
        out_shape=jax.ShapeDtypeStruct(g.shape, g.dtype),
        in_specs=[pl.BlockSpec(memory_space=pltpu.VMEM)] * 4 + [pl.BlockSpec(memory_space=pl.ANY)],
        out_specs=pl.BlockSpec((D, 128), lambda i: (0, 8)),
        input_output_aliases={4: 0},
        cost_estimate=pl.CostEstimate(flops=10**9, bytes_accessed=0, transcendentals=0),
        compiler_params=pltpu.CompilerParams(vmem_limit_bytes=VMEM_MB * 1024 * 1024),
    )(*packs, g)


def leave_kernel(place, grad, own, a, p0, p1, p2, p3, xq, stat, gains, out):
    sums = p0[:, D:] + p1[:, D:] + p2[:, D:] + p3[:, D:]
    sums = jnp.concatenate([sums, jnp.zeros((120, OWN), F32)], axis=0).T
    m1, m2 = sums[:, 0:1], sums[:, 1:2]
    e = own[0].astype(F32) + a[...].astype(F32)
    e = e * gains[0:1, block(place, 0)]
    y = grad[...] + own_rows(stat)[:, 1:2] * (e - m1 - xq[...] * m2)
    out[...] = y.astype(BF)


def output_kernel(stream, own, a, b, c, out):
    y = stream[...] + own[0].astype(F32) + a[...].astype(F32)
    out[...] = (y + b[...].astype(F32) + c[...].astype(F32)).astype(BF)


def mp_gather(x):
    far = turn_by(x, "yl", 1)
    return x, turn_by(x, "c", 1), far, turn_by(far, "c", 1)


def mp_turn(x, slot):
    return lax.ppermute(x, ("yl", "c"), [(i, i ^ slot) for i in range(4)])


def mp_terms(slots):
    return [slots, *(mp_turn(slots[s], s) for s in (1, 2, 3))]


def mp_reduce(even, odd):
    return (even.astype(F32) + turn_by(odd, "c", 1).astype(F32)).astype(BF)


def mp_sum(even, odd):
    half = mp_reduce(even, odd)
    far = turn_by(half, "yl", 1)
    return half, far, turn_by(half, "c", 1), turn_by(far, "c", 1)


def dp_turn(x, by):
    pairs = [(i, i + by) for i in range(32) if 0 <= i + by < 32]
    return lax.ppermute(x, ("z", "x", "yh"), pairs)


def rope_tables(place):
    rows = []
    for b in range(4):
        r = ROWS[b]
        rows.append((place * r + jnp.arange(r + 128, dtype=jnp.int32) - REACH) % LEN)
    position = jnp.concatenate(rows).astype(F32)
    frequency = 1.0 / 10000.0 ** (jnp.arange(0, HEAD_DIM, 2, dtype=F32) / HEAD_DIM)
    angles = position[:, None] * frequency[None, :]
    c, s = jnp.cos(angles), jnp.sin(angles)
    return jnp.concatenate([c, c, c, c], axis=1), jnp.concatenate([-s, s, -s, s], axis=1)


def body(block_input, cotangent, norm_gain, w_qkv, w_out, w_in, w_down):
    mp = lax.axis_index("yl") * 2 + lax.axis_index("c")
    dp = (lax.axis_index("z") * 4 + lax.axis_index("x")) * 2 + lax.axis_index("yh")
    place = jnp.stack([mp, dp]).astype(jnp.int32)

    gain_t = jnp.pad(norm_gain[0].T, ((0, 0), (0, 126)))
    shard0 = jnp.concatenate([w_qkv[0].reshape(32, 768), w_out[0].T, gain_t], axis=1)
    in0, in1, down_t = w_in[0, :, 0], w_in[0, :, 1], w_down[0].T
    shard1 = jnp.concatenate(
        [in0[:, :MAIN], in1[:, :MAIN], down_t[:, :MAIN]]
        + [in0[:, MAIN:], in1[:, MAIN:], down_t[:, MAIN:], jnp.zeros((32, 128 - 3 * TAIL), BF)],
        axis=1,
    )
    shard = jnp.concatenate([shard0, shard1], axis=1)
    lows = jnp.concatenate([block_input[o + r - 64 : o + r] for o, r in zip(OWN_AT, ROWS)], axis=0)
    highs = jnp.concatenate([block_input[o : o + 64] for o in OWN_AT], axis=0)
    lows, highs, shard = lax.optimization_barrier((lows, highs, shard))
    low, high = dp_turn(lows, 1), dp_turn(highs, -1)
    pair = turn_by(shard, "yh", 1)
    low, high, pair = lax.optimization_barrier((low, high, pair))
    first = lax.axis_index("yh") == 0
    pair = [jnp.where(first, shard, pair), jnp.where(first, pair, shard)]
    pair = jnp.concatenate(pair, axis=0)
    spread = jnp.broadcast_to(pair[None, :, :1152], (16, 64, 1152)).reshape(D, 1152)
    w0 = lax.all_to_all(spread, ("z", "x"), 0, 0, tiled=True)
    w1 = lax.all_gather(pair[:, 1152:], ("z", "x"), axis=0, tiled=True)
    x_slots = mp_gather(jnp.concatenate([block_input, low, high], axis=0))
    cos, sin = rope_tables(dp)

    xr, xo, stat1 = call(
        5, enter_kernel, [((EXT, D), BF), ((OWN, D), BF), ((EXT, 128), F32)], [], place, *x_slots
    )
    xr, cotangent = lax.optimization_barrier((xr, cotangent))
    xr, *c_slots = lax.optimization_barrier((xr, *mp_gather(cotangent)))
    slots = [((2, OWN, 256), BF)] * 2
    gains, normed1, qx, kx, vx, att, lse, *parts = call(
        10,
        attend_kernel,
        [((8, D), F32), ((OWN, D), BF), ((EXT, 256), BF), ((EXT, 256), BF), ((EXT, 256), BF)]
        + [((OWN, 256), BF), ((OWN, 128), F32)] + slots,
        [((EXT, D), BF), ((EXT, 256), F32)],
        place, xr, stat1, w0, cos, sin,
    )
    ct, stream, xhat2, rinv2, normed2, act, de0, de1, even, odd, gain2 = call(
        10,
        mlp_kernel,
        [
            ((OWN, D), BF), ((OWN, 256), F32), ((OWN, D), F32), ((OWN, 128), F32), ((OWN, D), BF),
            ((OWN, FFP), BF), ((OWN, FFP), BF), ((OWN, FFP), BF),
            *slots, ((1, D), F32),
        ],
        [((D, FFP), BF), ((D, FFP), BF), ((D, FFP), BF), ((OWN, D), F32)],
        place, xo, *mp_sum(*parts), gains, w1, *c_slots,
    )
    half = mp_reduce(even, odd)
    far = turn_by(half, "yl", 1)
    half_c = turn_by(half, "c", 1)
    down, g1 = call(
        9,
        mlp_grads_kernel,
        [((4, OWN, 256), BF), ((D, 2048), BF)],
        [((D, FFP), BF)],
        place, normed2, act, de0, de1, ct, columns(w1, 2, MAIN), columns(w1, 15, 128),
    )
    far, down, g1 = lax.optimization_barrier((far, down, g1))
    far_c = turn_by(far, "c", 1)
    g1 = scatter_sum(g1, "z")
    down = mp_terms(down)

    grad, gb, da, da_first, da_last = call(
        6,
        norm_back_kernel,
        [((OWN, 256), F32), ((OWN, D), BF), ((OWN, 256), BF)]
        + [((HALO + 16, 256), BF)] * 2,
        [((OWN, D), F32), ((OWN, 128), F32)],
        place, half, far, half_c, far_c, ct, xhat2, rinv2, gains, columns(w0, 3, 256), att, lse,
    )
    da_lo, da_hi = dp_turn(da_last, 1), dp_turn(da_first, -1)
    da_lo, da_hi, *down = lax.optimization_barrier((da_lo, da_hi, *down))
    go, dq, dk, dv = call(
        8,
        attend_back_kernel,
        [((D, 256), BF)] + [((OWN, 256), F32)] * 3,
        [],
        place, da, lse, gb, att, qx, kx, vx,
    )
    even, odd, pack, xq, raw = call(
        7,
        functools.partial(qkv_in_place, qkv_back_kernel),
        [*slots, ((8, PACK), F32), ((OWN, 256), F32), ((OWN, 768), BF)],
        [((OWN, 256), F32), ((OWN, 256), F32), ((1, D), F32)],
        place, dq, dk, dv, da_lo, da_hi, qx, kx, vx, cos, sin, xo, stat1, gains, gain2, columns(w0, 0, 768),
    )
    half = mp_reduce(even, odd)
    half, normed1 = lax.optimization_barrier((half, normed1))
    dn = [half, turn_by(half[1], "yl", 1)]
    packs = [pack, *(mp_turn(pack, s) for s in (1, 2, 3))]
    (g0,) = call(4, qkv_grads_kernel, [((D, 1152), BF)], [], normed1, raw, go)
    at = lax.axis_index("x")
    parts = [lax.dynamic_slice_in_dim(g1, ((at + k) % 4) * 64, 64, 0) for k in range(4)]
    g0, *rest = lax.optimization_barrier((g0, *dn, *packs, *parts))
    dn, packs, parts = rest[:2], rest[2:6], rest[6:]
    g1 = sum_over(parts, "x")
    g0 = with_gains(g0, packs)
    g0, *down = lax.optimization_barrier((g0, *down))
    (block_output,) = call(2, output_kernel, [((OWN, 256), BF)], [], stream, *down)
    g0 = sum_of(lax.all_to_all(g0, DP, 0, 0, tiled=True), 32)
    (input_grad,) = call(
        2, leave_kernel, [((OWN, 256), BF)], [],
        place, grad, *dn, *packs, xq, stat1, gains,
    )
    g1 = jnp.where(first, g1[:32], g1[32:]).astype(F32) + turn_by(
        jnp.where(first, g1[32:], g1[:32]), "yh", 1
    ).astype(F32)
    in0, in1, down_t = [
        jnp.concatenate(
            [g1[:, k * MAIN : k * MAIN + MAIN], g1[:, 3 * MAIN + k * TAIL : 3 * MAIN + k * TAIL + TAIL]],
            axis=1,
        )
        for k in range(3)
    ]
    return (
        block_output, input_grad, g0[:, 1024:1026].T[None], g0[:, :768].reshape(1, 32, 3, 256),
        g0[:, 768:1024].T[None], jnp.stack([in0, in1], axis=1)[None], down_t.T[None],
    )


def qkv_in_place(inner, place, dq, dk, dv, *refs):
    *refs, dks, dvs, gsum = refs
    dks[...] = dk[...]
    dvs[...] = dv[...]
    inner(place, dq, dks, dvs, *refs, gsum)


def solution(mesh):
    fine = Mesh(mesh.devices.reshape(4, 4, 2, 2, 2), ("z", "x", "yh", "yl", "c"))
    dp, mp = ("z", "x", "yh"), ("yl", "c")
    return jax.shard_map(
        body,
        mesh=fine,
        in_specs=(
            P(dp, mp),
            P(dp, mp),
            P(None, None, dp),
            P(None, dp, None, mp),
            P(None, mp, dp),
            P(None, dp, None, mp),
            P(None, mp, dp),
        ),
        out_specs=(
            P(dp, mp),
            P(dp, mp),
            P(None, None, dp),
            P(None, dp, None, mp),
            P(None, mp, dp),
            P(None, dp, None, mp),
            P(None, mp, dp),
        ),
        check_vma=False,
    )
```
